32 devices in a mesh: band: 8 (over z, y), domain: 4 (over x, core).
Axes of the slice: x: 2, y: 2, z: 4, core: 2. Of those that a mesh axis runs over, the one named last changes fastest.
Arguments:
- orbitals: bfloat16 [1024, 8, 5120], P('band', 'domain'), may hold values from -6 to 6
- boundary: bfloat16 [1024, 4, 5120], P('band'), may hold values from -6 to 6
- potential: bfloat16 [8, 5120], P('domain'), may hold values from 0 to 2
Outputs:
- correlation: float32 [1024, 1024], P('band', 'domain')
- projected: float32 [1024, 1024], P('band', 'domain')
The draws below stay inside these ranges and needn't reach their ends.
All inputs are finite; a program needn't handle non-finite values.
Results may differ from the reference program's by a relative error of at most 0.0012.
Values may be sent and summed in bfloat16 or wider, within the bound.
A program may use at most 128 MiB of HBM per device.

```python
import math
import jax
import jax.numpy as jnp
from jax import lax

NORB = 1024
NX = 160
NY = 32
DEGREE = 4
NZ = 8
PLANE = 5120


def level_of(rng, dims, split, least, largest):
    def one(axis_at, parts):
        draws = jax.random.uniform(jax.random.fold_in(jax.random.fold_in(rng, 6), axis_at), (parts,), jnp.float32, least / len(split), largest / len(split))
        return jnp.repeat(jnp.exp(draws), dims[axis_at] // parts).reshape((-1,) + (1,) * (len(dims) - axis_at - 1))

    level = one(*split[0])
    for cut in split[1:]:
        level = level * one(*cut)
    return level


def noise(stream_key, dims, deviation, reach, cuts=(), dtype=jnp.bfloat16):
    array = jax.random.normal(stream_key, dims, jnp.float32) * deviation
    if len(cuts) > 0:
        array = level_of(stream_key, dims, cuts, -0.22, 0.18) * array
    return jnp.clip(array, min=-reach, max=reach).astype(dtype)


def setup_inputs(seed: int = 0) -> dict:
    keys = jax.random.split(jax.random.key(seed), 4)
    return {
        "orbitals": noise(keys[0], (NORB, NZ, PLANE), 1.0, 6.0, ((0, 8), (1, 4))),
        "boundary": noise(keys[1], (NORB, 4, PLANE), 1.0, 6.0, ((0, 8),)),
        "potential": jnp.clip(2.0 * jax.random.uniform(keys[2], (NZ, PLANE), jnp.float32) ** level_of(keys[2], (NZ, PLANE), ((0, 4),), -0.2, 0.2), 0.0, 2.0).astype(jnp.bfloat16),
    }


filter_center = 5.5
filter_radius = 4.5


def second_diff(values, axis_pos):
    near = jnp.roll(values, 1, axis_pos) + jnp.roll(values, -1, axis_pos)
    far = jnp.roll(values, 2, axis_pos) + jnp.roll(values, -2, axis_pos)
    return (16.0 * near - far - 30.0 * values) / 12.0


def plane_part(values):
    shaped = values.reshape(values.shape[:-1] + (NY, NX))
    total = second_diff(shaped, -1) + second_diff(shaped, -2)
    return total.reshape(values.shape)


def hamiltonian(padded, potential):
    middle = padded[:, 2:-2]
    z_part = (16.0 * (padded[:, 1:-3] + padded[:, 3:-1]) - (padded[:, :-4] + padded[:, 4:]) - 30.0 * middle) / 12.0
    laplace = z_part + plane_part(middle)
    return -0.5 * laplace + potential.astype(jnp.float32) * middle


def chebyshev(apply_ham, orb_block):
    earlier = orb_block
    current = ((apply_ham(orb_block) - filter_center * orb_block.astype(jnp.float32)) / filter_radius).astype(jnp.bfloat16)
    for degree_step in range(DEGREE - 1):
        following = 2.0 * (apply_ham(current) - filter_center * current.astype(jnp.float32)) / filter_radius
        following = (following - earlier.astype(jnp.float32)).astype(jnp.bfloat16)
        earlier, current = current, following
    return current, apply_ham(current).astype(jnp.bfloat16)


def reference(orbitals, boundary, potential):
    group_size = math.gcd(NORB, 64)

    def one_group(pieces):
        orb_block, rim_planes = pieces

        def apply_ham(values):
            padded = jnp.concatenate([rim_planes[:, 0:2], values, rim_planes[:, 2:4]], axis=1).astype(jnp.float32)
            return hamiltonian(padded, potential)

        return chebyshev(apply_ham, orb_block)

    grouped = (orbitals.reshape(NORB // group_size, group_size, NZ, NY * NX),
               boundary.reshape(NORB // group_size, group_size, 4, NY * NX))
    filtered, applied = lax.map(one_group, grouped)
    filtered = filtered.reshape(NORB, NZ * NY * NX).astype(jnp.float32)
    applied = applied.reshape(NORB, NZ * NY * NX).astype(jnp.float32)
    total_cells = NZ * NY * NX
    correlation = jnp.dot(filtered, filtered.T, precision=lax.Precision.HIGHEST) / total_cells
    projected = jnp.dot(filtered, applied.T, precision=lax.Precision.HIGHEST) / total_cells
    return correlation, projected
```

```python
import functools

import jax
import jax.numpy as jnp
from jax import lax
from jax.experimental import pallas as pl
from jax.experimental.pallas import tpu as pltpu
from jax.sharding import PartitionSpec as P

NX = 160
NY = 32
NZ_DEV = 2
DEGREE = 4
LANES = 128
PAD = 8
YB = 8
GAP = 2


filter_center = 5.5
filter_radius = 4.5


def padded_2(cells, sides, width):
    for axis, dim in sides:
        count = lax.axis_size(axis)
        ends = count - 1
        head = lax.slice_in_dim(cells, 0, width, axis=dim)
        tail = lax.slice_in_dim(cells, cells.shape[dim] - width, cells.shape[dim], axis=dim)
        cells = jnp.concatenate(
            [
                lax.ppermute(tail, axis, [(i, (i + 1) % count) for i in range(ends)]),
                cells,
                lax.ppermute(head, axis, [((i + 1) % count, i) for i in range(ends)]),
            ],
            axis=dim,
        )
    return cells


def second_diff(values, axis_pos):
    near = jnp.roll(values, 1, axis_pos) + jnp.roll(values, -1, axis_pos)
    far = jnp.roll(values, 2, axis_pos) + jnp.roll(values, -2, axis_pos)
    return (16.0 * near - far - 30.0 * values) / 12.0


def plane_part(values):
    shaped = values.reshape(values.shape[:-1] + (NY, NX))
    total = second_diff(shaped, -1) + second_diff(shaped, -2)
    return total.reshape(values.shape)


def hamiltonian(padded, potential):
    middle = padded[:, 2:-2]
    z_part = (
        16.0 * (padded[:, 1:-3] + padded[:, 3:-1])
        - (padded[:, :-4] + padded[:, 4:])
        - 30.0 * middle
    ) / 12.0
    laplace = z_part + plane_part(middle)
    return -0.5 * laplace + potential.astype(jnp.float32) * middle


def chebyshev(apply_ham, orb_block):
    earlier = orb_block
    current = (
        (apply_ham(orb_block) - filter_center * orb_block.astype(jnp.float32)) / filter_radius
    ).astype(jnp.bfloat16)
    for degree_step in range(DEGREE - 1):
        following = (
            2.0 * (apply_ham(current) - filter_center * current.astype(jnp.float32)) / filter_radius
        )
        following = (following - earlier.astype(jnp.float32)).astype(jnp.bfloat16)
        earlier, current = (current, following)
    return (current, apply_ham(current).astype(jnp.bfloat16))


def per_device(orbitals, boundary, potential):
    orb_count = orbitals.shape[0]
    domain_pos = lax.axis_index("domain")
    domain_count = lax.axis_size("domain")
    last_pos = domain_count - 1

    def apply_ham(values):
        padded = padded_2(values, (("domain", 1),), 2)
        lower_rim = jnp.where(domain_pos == 0, boundary[:, 0:2], padded[:, 0:2])
        upper_rim = jnp.where(domain_pos == last_pos, boundary[:, 2:4], padded[:, -2:])
        padded = jnp.concatenate([lower_rim, padded[:, 2:-2], upper_rim], axis=1).astype(
            jnp.float32
        )
        return hamiltonian(padded, potential)

    filtered, applied = chebyshev(apply_ham, orbitals)
    filtered = filtered.reshape(orb_count, -1)
    applied = applied.reshape(orb_count, -1)
    cell_y, cell_h = (
        lax.all_to_all(filtered, "band", split_axis=1, concat_axis=0, tiled=True),
        lax.all_to_all(applied, "band", split_axis=1, concat_axis=0, tiled=True),
    )
    cell_y, cell_h = (
        lax.all_gather(cell_y, "domain", axis=1, tiled=True),
        lax.all_gather(cell_h, "domain", axis=1, tiled=True),
    )
    column_count = cell_y.shape[0] // domain_count
    column_y = lax.dynamic_slice_in_dim(cell_y, domain_pos * column_count, column_count, 0)
    column_h = lax.dynamic_slice_in_dim(cell_h, domain_pos * column_count, column_count, 0)
    contract_dims = (((1,), (1,)), ((), ()))
    with_y = lax.dot_general(cell_y, column_y, contract_dims, preferred_element_type=jnp.float32)
    with_h = lax.dot_general(cell_y, column_h, contract_dims, preferred_element_type=jnp.float32)
    summed = lax.psum_scatter(
        jnp.concatenate([with_y, with_h], axis=1), "band", scatter_dimension=0, tiled=True
    )
    total_cells = NZ_DEV * NY * NX * domain_count
    correlation = summed[:, :column_count] / total_cells
    projected = summed[:, column_count:] / total_cells
    return (correlation, projected)


SCALE = 2.0 / filter_radius
K_NEAR = SCALE * 16.0 / 24.0
K_FAR = SCALE / 24.0


def plane_in(src):
    group = YB * NX
    rows = jnp.concatenate(
        [src[:, g * group : (g + 1) * group].astype(jnp.float32) for g in range(NY // YB)], axis=0
    )
    return rows.T.reshape(YB, NX, LANES)


def fill_rims(buf, z):
    for yi in range(YB):
        buf[z, yi + GAP, PAD - 2 : PAD] = buf[z, yi + GAP, PAD + NX - 2 : PAD + NX]
        buf[z, yi + GAP, PAD + NX : PAD + NX + 2] = buf[z, yi + GAP, PAD : PAD + 2]
    turn = LANES // (NY // YB)
    for k in range(GAP):
        low = buf[z, YB + k, PAD : PAD + NX]
        buf[z, k, PAD : PAD + NX] = pltpu.roll(low, turn, 1)
        high = buf[z, GAP + k, PAD : PAD + NX]
        buf[z, GAP + YB + k, PAD : PAD + NX] = pltpu.roll(high, LANES - turn, 1)


def apply_step(cur, out, coef, kind, planes):
    chunk = 40

    @pl.loop(0, YB)
    def _(yi):
        for x0 in range(PAD, PAD + NX, chunk):
            here = pl.ds(x0, chunk)
            mids = [cur[z, yi + GAP, here] for z in range(planes + 4)]
            for z in range(planes):
                zc = z + 2
                v = mids[zc]
                near = (
                    (mids[zc - 1] + mids[zc + 1])
                    + (cur[zc, yi + 1, here] + cur[zc, yi + 3, here])
                    + (cur[zc, yi + GAP, pl.ds(x0 - 1, chunk)] + cur[zc, yi + GAP, pl.ds(x0 + 1, chunk)])
                )
                far = (
                    (mids[zc - 2] + mids[zc + 2])
                    + (cur[zc, yi, here] + cur[zc, yi + 4, here])
                    + (cur[zc, yi + GAP, pl.ds(x0 - 2, chunk)] + cur[zc, yi + GAP, pl.ds(x0 + 2, chunk)])
                )
                r = coef[z, yi, pl.ds(x0 - PAD, chunk)] * v - K_NEAR * near + K_FAR * far
                if kind == "first":
                    r = 0.5 * r
                elif kind == "next":
                    r = r - out[zc, yi + GAP, here]
                else:
                    r = r * (1.0 / SCALE) + filter_center * v
                out[zc, yi + GAP, here] = r.astype(jnp.bfloat16).astype(jnp.float32)


def filter_kernel(orb_ref, rim_ref, pot_ref, f_ref, a_ref, buf_a, buf_b, coef):
    planes = orb_ref.shape[0]
    count = orb_ref.shape[1]

    for k in range(4):
        z = k if k < 2 else planes + k
        rim = plane_in(rim_ref[k])
        buf_a[z, GAP : GAP + YB, PAD : PAD + NX] = rim
        buf_b[z, GAP : GAP + YB, PAD : PAD + NX] = rim

    @pl.loop(0, planes)
    def _(z):
        row = pot_ref[z].astype(jnp.float32)
        spread = jnp.broadcast_to((row - 1.75) * SCALE, (count, row.shape[-1]))
        coef[z] = plane_in(spread)
        buf_a[z + 2, GAP : GAP + YB, PAD : PAD + NX] = plane_in(orb_ref[z])
        fill_rims(buf_a, z + 2)

    def rims(buf):
        @pl.loop(0, planes)
        def _(z):
            fill_rims(buf, z + 2)

    def emit(buf, ref):
        @pl.loop(0, planes)
        def _(z):
            cells = buf[z + 2, GAP : GAP + YB, PAD : PAD + NX].reshape(YB * NX, LANES)
            ref[z] = cells.T.astype(jnp.bfloat16)

    cur, other = buf_a, buf_b
    apply_step(cur, other, coef, "first", planes)
    for _ in range(DEGREE - 1):
        cur, other = other, cur
        rims(cur)
        apply_step(cur, other, coef, "next", planes)
    cur, other = other, cur
    rims(cur)
    emit(cur, f_ref)
    apply_step(cur, other, coef, "last", planes)
    emit(other, a_ref)


def run_filter(orb, rim, pot):
    planes = orb.shape[0]
    out = jax.ShapeDtypeStruct((planes, LANES, YB * NX), jnp.bfloat16)
    whole = pl.BlockSpec(memory_space=pltpu.VMEM)
    field = pltpu.VMEM((planes + 4, YB + 2 * GAP, NX + 2 * PAD, LANES), jnp.float32)
    return pl.pallas_call(
        filter_kernel,
        out_shape=(out, out),
        in_specs=[whole] * 3,
        out_specs=(whole, whole),
        scratch_shapes=[field, field, pltpu.VMEM((planes, YB, NX, LANES), jnp.float32)],
        compiler_params=pltpu.CompilerParams(vmem_limit_bytes=56 * 1024 * 1024),
        name="chebyshev",
    )(orb, rim, pot[:, None])


def gram_kernel(all_ref, f_ref, a_ref, out_ref):
    parts, bands, groups, count, cells = all_ref.shape
    rows = bands * count

    @pl.loop(0, parts)
    def _(d):
        for ref, at in ((f_ref, 0), (a_ref, rows)):
            total = jnp.zeros((rows, rows), jnp.float32)
            for g in range(groups):
                total += lax.dot_general(
                    all_ref[d, :, g].reshape(rows, cells),
                    ref[:, g].reshape(rows, cells),
                    (((1,), (1,)), ((), ())),
                    preferred_element_type=jnp.float32,
                )
            out_ref[:, d, :, at : at + rows] = total.reshape(bands, count, rows)


def run_gram(everyone, own_f, own_a):
    parts, bands, groups, count, cells = everyone.shape
    whole = pl.BlockSpec(memory_space=pltpu.VMEM)
    return pl.pallas_call(
        gram_kernel,
        out_shape=jax.ShapeDtypeStruct((bands, parts, count, 2 * bands * count), jnp.float32),
        in_specs=[whole] * 3,
        out_specs=whole,
        compiler_params=pltpu.CompilerParams(vmem_limit_bytes=56 * 1024 * 1024),
        name="gram",
    )(everyone, own_f, own_a)


def whole_orbitals(orbitals, boundary, potential):
    orb_count, planes_here, plane = orbitals.shape
    parts = lax.axis_size("domain")
    bands = lax.axis_size("band")
    part = lax.axis_index("domain")
    count = orb_count // parts

    split = orbitals.reshape(parts, count, planes_here, plane).transpose(0, 2, 1, 3)
    mine = lax.all_to_all(split, "domain", split_axis=0, concat_axis=0, tiled=True)
    mine = mine.reshape(parts * planes_here, count, plane)
    rim = lax.dynamic_slice_in_dim(boundary, part * count, count, 0).transpose(1, 0, 2)
    pot = lax.all_gather(potential, "domain", axis=0, tiled=True)
    f, a = run_filter(mine, rim, pot)

    groups = LANES // count
    shape = (bands, groups, count, f.shape[-1])
    f = lax.all_to_all(f, "band", split_axis=0, concat_axis=0, tiled=True).reshape(shape)
    everyone = lax.all_gather(f, "domain", axis=0)
    a = lax.all_to_all(a, "band", split_axis=0, concat_axis=0, tiled=True).reshape(shape)
    partial = run_gram(everyone, f, a)
    summed = lax.psum_scatter(
        partial.reshape(bands * orb_count, -1), "band", scatter_dimension=0, tiled=True
    )
    total_cells = parts * planes_here * plane
    summed = summed.reshape(orb_count, 2, parts, bands // parts, count) / total_cells
    summed = lax.all_to_all(
        summed.transpose(2, 1, 0, 3, 4), "domain", split_axis=0, concat_axis=0, tiled=True
    )
    summed = summed.transpose(1, 2, 3, 0, 4).reshape(2, orb_count, -1)
    return summed[0], summed[1]


def solution(mesh):
    parts, bands = mesh.shape["domain"], mesh.shape["band"]

    def body(orbitals, boundary, potential):
        fits = (
            orbitals.shape[0] * (NY // YB) == LANES * parts
            and orbitals.shape[1] * parts == bands
            and bands % parts == 0
        )
        return (whole_orbitals if fits else per_device)(orbitals, boundary, potential)

    return jax.shard_map(
        body,
        mesh=mesh,
        in_specs=(P("band", "domain", None), P("band", None, None), P("domain", None)),
        out_specs=(P("band", "domain"), P("band", "domain")),
        check_vma=False,
    )
```

```python
import functools

import jax
import jax.numpy as jnp
from jax import lax
from jax.experimental import pallas as pl
from jax.experimental.pallas import tpu as pltpu
from jax.sharding import PartitionSpec as P

NX = 160
NY = 32
NZ_DEV = 2
DEGREE = 4
LANES = 128
PAD = 8
YB = 8
GAP = 2
MESH = pl.DeviceIdType.MESH


filter_center = 5.5
filter_radius = 4.5


def padded_2(cells, sides, width):
    for axis, dim in sides:
        count = lax.axis_size(axis)
        ends = count - 1
        head = lax.slice_in_dim(cells, 0, width, axis=dim)
        tail = lax.slice_in_dim(cells, cells.shape[dim] - width, cells.shape[dim], axis=dim)
        cells = jnp.concatenate(
            [
                lax.ppermute(tail, axis, [(i, (i + 1) % count) for i in range(ends)]),
                cells,
                lax.ppermute(head, axis, [((i + 1) % count, i) for i in range(ends)]),
            ],
            axis=dim,
        )
    return cells


def second_diff(values, axis_pos):
    near = jnp.roll(values, 1, axis_pos) + jnp.roll(values, -1, axis_pos)
    far = jnp.roll(values, 2, axis_pos) + jnp.roll(values, -2, axis_pos)
    return (16.0 * near - far - 30.0 * values) / 12.0


def plane_part(values):
    shaped = values.reshape(values.shape[:-1] + (NY, NX))
    total = second_diff(shaped, -1) + second_diff(shaped, -2)
    return total.reshape(values.shape)


def hamiltonian(padded, potential):
    middle = padded[:, 2:-2]
    z_part = (
        16.0 * (padded[:, 1:-3] + padded[:, 3:-1])
        - (padded[:, :-4] + padded[:, 4:])
        - 30.0 * middle
    ) / 12.0
    laplace = z_part + plane_part(middle)
    return -0.5 * laplace + potential.astype(jnp.float32) * middle


def chebyshev(apply_ham, orb_block):
    earlier = orb_block
    current = (
        (apply_ham(orb_block) - filter_center * orb_block.astype(jnp.float32)) / filter_radius
    ).astype(jnp.bfloat16)
    for degree_step in range(DEGREE - 1):
        following = (
            2.0 * (apply_ham(current) - filter_center * current.astype(jnp.float32)) / filter_radius
        )
        following = (following - earlier.astype(jnp.float32)).astype(jnp.bfloat16)
        earlier, current = (current, following)
    return (current, apply_ham(current).astype(jnp.bfloat16))


def per_device(orbitals, boundary, potential):
    orb_count = orbitals.shape[0]
    domain_pos = lax.axis_index("domain")
    domain_count = lax.axis_size("domain")
    last_pos = domain_count - 1

    def apply_ham(values):
        padded = padded_2(values, (("domain", 1),), 2)
        lower_rim = jnp.where(domain_pos == 0, boundary[:, 0:2], padded[:, 0:2])
        upper_rim = jnp.where(domain_pos == last_pos, boundary[:, 2:4], padded[:, -2:])
        padded = jnp.concatenate([lower_rim, padded[:, 2:-2], upper_rim], axis=1).astype(
            jnp.float32
        )
        return hamiltonian(padded, potential)

    filtered, applied = chebyshev(apply_ham, orbitals)
    filtered = filtered.reshape(orb_count, -1)
    applied = applied.reshape(orb_count, -1)
    cell_y, cell_h = (
        lax.all_to_all(filtered, "band", split_axis=1, concat_axis=0, tiled=True),
        lax.all_to_all(applied, "band", split_axis=1, concat_axis=0, tiled=True),
    )
    cell_y, cell_h = (
        lax.all_gather(cell_y, "domain", axis=1, tiled=True),
        lax.all_gather(cell_h, "domain", axis=1, tiled=True),
    )
    column_count = cell_y.shape[0] // domain_count
    column_y = lax.dynamic_slice_in_dim(cell_y, domain_pos * column_count, column_count, 0)
    column_h = lax.dynamic_slice_in_dim(cell_h, domain_pos * column_count, column_count, 0)
    contract_dims = (((1,), (1,)), ((), ()))
    with_y = lax.dot_general(cell_y, column_y, contract_dims, preferred_element_type=jnp.float32)
    with_h = lax.dot_general(cell_y, column_h, contract_dims, preferred_element_type=jnp.float32)
    summed = lax.psum_scatter(
        jnp.concatenate([with_y, with_h], axis=1), "band", scatter_dimension=0, tiled=True
    )
    total_cells = NZ_DEV * NY * NX * domain_count
    correlation = summed[:, :column_count] / total_cells
    projected = summed[:, column_count:] / total_cells
    return (correlation, projected)


SCALE = 2.0 / filter_radius
K_NEAR = SCALE * 16.0 / 24.0
K_FAR = SCALE / 24.0


def plane_in(src):
    group = YB * NX
    rows = jnp.concatenate(
        [src[:, g * group : (g + 1) * group].astype(jnp.float32) for g in range(NY // YB)], axis=0
    )
    return rows.T.reshape(YB, NX, LANES)


def fill_rims(buf, z):
    for yi in range(YB):
        buf[z, yi + GAP, PAD - 2 : PAD] = buf[z, yi + GAP, PAD + NX - 2 : PAD + NX]
        buf[z, yi + GAP, PAD + NX : PAD + NX + 2] = buf[z, yi + GAP, PAD : PAD + 2]
    turn = LANES // (NY // YB)
    for k in range(GAP):
        low = buf[z, YB + k, PAD : PAD + NX]
        buf[z, k, PAD : PAD + NX] = pltpu.roll(low, turn, 1)
        high = buf[z, GAP + k, PAD : PAD + NX]
        buf[z, GAP + YB + k, PAD : PAD + NX] = pltpu.roll(high, LANES - turn, 1)


def apply_step(cur, out, coef, kind, planes):
    chunk = 40

    @pl.loop(0, YB)
    def _(yi):
        for x0 in range(PAD, PAD + NX, chunk):
            here = pl.ds(x0, chunk)
            mids = [cur[z, yi + GAP, here] for z in range(planes + 4)]
            for z in range(planes):
                zc = z + 2
                v = mids[zc]
                near = (
                    (mids[zc - 1] + mids[zc + 1])
                    + (cur[zc, yi + 1, here] + cur[zc, yi + 3, here])
                    + (cur[zc, yi + GAP, pl.ds(x0 - 1, chunk)] + cur[zc, yi + GAP, pl.ds(x0 + 1, chunk)])
                )
                far = (
                    (mids[zc - 2] + mids[zc + 2])
                    + (cur[zc, yi, here] + cur[zc, yi + 4, here])
                    + (cur[zc, yi + GAP, pl.ds(x0 - 2, chunk)] + cur[zc, yi + GAP, pl.ds(x0 + 2, chunk)])
                )
                r = coef[z, yi, pl.ds(x0 - PAD, chunk)] * v - K_NEAR * near + K_FAR * far
                if kind == "first":
                    r = 0.5 * r
                elif kind == "next":
                    r = r - out[zc, yi + GAP, here]
                else:
                    r = r * (1.0 / SCALE) + filter_center * v
                out[zc, yi + GAP, here] = r.astype(jnp.bfloat16).astype(jnp.float32)


def filter_kernel(orb_ref, rim_ref, pot_ref, f_ref, a_ref, buf_a, buf_b, coef):
    planes = orb_ref.shape[0]
    count = orb_ref.shape[1]

    for k in range(4):
        z = k if k < 2 else planes + k
        rim = plane_in(rim_ref[k])
        buf_a[z, GAP : GAP + YB, PAD : PAD + NX] = rim
        buf_b[z, GAP : GAP + YB, PAD : PAD + NX] = rim

    @pl.loop(0, planes)
    def _(z):
        row = pot_ref[z].astype(jnp.float32)
        spread = jnp.broadcast_to((row - 1.75) * SCALE, (count, row.shape[-1]))
        coef[z] = plane_in(spread)
        buf_a[z + 2, GAP : GAP + YB, PAD : PAD + NX] = plane_in(orb_ref[z])
        fill_rims(buf_a, z + 2)

    def rims(buf):
        @pl.loop(0, planes)
        def _(z):
            fill_rims(buf, z + 2)

    def emit(buf, ref):
        @pl.loop(0, planes)
        def _(z):
            cells = buf[z + 2, GAP : GAP + YB, PAD : PAD + NX].reshape(YB * NX, LANES)
            ref[z] = cells.T.astype(jnp.bfloat16)

    cur, other = buf_a, buf_b
    apply_step(cur, other, coef, "first", planes)
    for _ in range(DEGREE - 1):
        cur, other = other, cur
        rims(cur)
        apply_step(cur, other, coef, "next", planes)
    cur, other = other, cur
    rims(cur)
    emit(cur, f_ref)
    apply_step(cur, other, coef, "last", planes)
    emit(other, a_ref)


def run_filter(orb, rim, pot):
    planes = orb.shape[0]
    out = jax.ShapeDtypeStruct((planes, LANES, YB * NX), jnp.bfloat16)
    whole = pl.BlockSpec(memory_space=pltpu.VMEM)
    field = pltpu.VMEM((planes + 4, YB + 2 * GAP, NX + 2 * PAD, LANES), jnp.float32)
    return pl.pallas_call(
        filter_kernel,
        out_shape=(out, out),
        in_specs=[whole] * 3,
        out_specs=(whole, whole),
        scratch_shapes=[field, field, pltpu.VMEM((planes, YB, NX, LANES), jnp.float32)],
        compiler_params=pltpu.CompilerParams(vmem_limit_bytes=56 * 1024 * 1024),
        name="chebyshev",
    )(orb, rim, pot[:, None])


def meet_all(bands, parts, band, part):
    barrier = pltpu.get_barrier_semaphore()
    total = bands * parts
    me = band * parts + part

    @pl.loop(1, total)
    def _(o):
        t = lax.rem(me + o, total)
        pl.semaphore_signal(
            barrier, inc=1, device_id=(t // parts, lax.rem(t, parts)), device_id_type=MESH
        )

    pl.semaphore_wait(barrier, total - 1)


def gram_kernel(
    bands, parts, total_cells,
    f_ref, a_ref, c_ref, p_ref,
    all_f, own_a, blocks, landed,
    f_send, f_recv, a_send, a_recv, x_send, mate_send, local_sem, b_send, b_recv,
):
    band, part = lax.axis_index("band"), lax.axis_index("domain")
    lanes, cells = f_ref.shape[1:]
    count = blocks.shape[2] // parts
    groups = lanes // count
    rows = bands * count
    wide = 2 * rows // parts
    mate = part + 1 - 2 * lax.rem(part, 2)
    across = lax.rem(part + 2, parts)
    across_mate = lax.rem(mate + 2, parts)
    meet_all(bands, parts, band, part)

    def band_copy(src, dst, send, recv, o, incoming):
        peer = lax.rem(band + o, bands)
        source = lax.rem(band - o + bands, bands)
        slot = source if incoming else band
        return pltpu.make_async_remote_copy(
            src_ref=src.at[peer], dst_ref=dst.at[slot], send_sem=send.at[o],
            recv_sem=recv.at[slot], device_id=(peer, part), device_id_type=MESH,
        )

    def f_copy(o, incoming):
        return band_copy(f_ref, all_f.at[part], f_send, f_recv.at[part], o, incoming)

    def a_copy(o, incoming):
        return band_copy(a_ref, own_a, a_send, a_recv, o, incoming)

    def part_copy(owner, to, slot, send):
        return pltpu.make_async_remote_copy(
            src_ref=all_f.at[owner, slot], dst_ref=all_f.at[owner, slot], send_sem=send.at[slot],
            recv_sem=f_recv.at[owner, slot], device_id=(band, to), device_id_type=MESH,
        )

    keep_f = pltpu.make_async_copy(f_ref.at[band], all_f.at[part, band], local_sem.at[0])
    keep_a = pltpu.make_async_copy(a_ref.at[band], own_a.at[band], local_sem.at[1])
    keep_f.start()
    keep_a.start()

    @pl.loop(1, bands)
    def _(o):
        f_copy(o, False).start()

    keep_f.wait()
    part_copy(part, across, band, x_send).start()
    part_copy(part, mate, band, mate_send.at[0]).start()

    @pl.loop(1, bands)
    def _(o):
        a_copy(o, False).start()

    @pl.loop(1, bands)
    def _(o):
        slot = lax.rem(band - o + bands, bands)
        f_copy(o, True).wait_recv()
        part_copy(part, across, slot, x_send).start()
        part_copy(part, mate, slot, mate_send.at[0]).start()

    @pl.loop(0, bands)
    def _(o):
        slot = lax.rem(band - o + bands, bands)
        part_copy(across, mate, slot, mate_send.at[1]).wait_recv()
        part_copy(across, mate, slot, mate_send.at[1]).start()

    keep_a.wait()

    @pl.loop(1, bands)
    def _(o):
        a_copy(o, True).wait_recv()

    def add_rows(owner):
        total = jnp.zeros((rows, 2 * rows), jnp.float32)
        for g in range(groups):
            at = slice(g * count, (g + 1) * count)
            sides = []
            for k in range(parts):
                two = slice(k * bands // parts, (k + 1) * bands // parts)
                sides.append(all_f[part, two, at].reshape(wide // 2, cells))
                sides.append(own_a[two, at].reshape(wide // 2, cells))
            total += lax.dot_general(
                all_f[owner, :, at].reshape(rows, cells),
                jnp.concatenate(sides, axis=0),
                (((1,), (1,)), ((), ())),
                preferred_element_type=jnp.float32,
            )
        for k in range(parts):
            blocks[:, k, pl.ds(pl.multiple_of(owner * count, count), count)] = total[
                :, k * wide : (k + 1) * wide
            ].reshape(bands, count, wide)

    @pl.loop(0, bands)
    def _(slot):
        part_copy(mate, part, slot, mate_send.at[0]).wait_recv()
        part_copy(across_mate, part, slot, mate_send.at[1]).wait_recv()

    @pl.loop(0, parts)
    def _(k):
        add_rows(k)

    me = band * parts + part
    total_devices = bands * parts

    def block_copy(o, incoming):
        t = lax.rem(me + o, total_devices)
        source = lax.rem(me - o + total_devices, total_devices)
        slot = source if incoming else me
        return pltpu.make_async_remote_copy(
            src_ref=blocks.at[t // parts, lax.rem(t, parts)], dst_ref=landed.at[slot],
            send_sem=b_send.at[o], recv_sem=b_recv.at[slot],
            device_id=(t // parts, lax.rem(t, parts)), device_id_type=MESH,
        )

    @pl.loop(1, total_devices)
    def _(o):
        block_copy(o, False).start()

    keep = pltpu.make_async_copy(blocks.at[band, part], landed.at[me], local_sem.at[0])
    keep.start()
    keep.wait()

    @pl.loop(1, total_devices)
    def _(o):
        block_copy(o, True).wait_recv()

    sums = []
    for d in range(parts):
        total = landed[d]
        for b in range(1, bands):
            total = total + landed[b * parts + d]
        sums.append(total * (1.0 / total_cells))
    for ref, at in ((c_ref, 0), (p_ref, wide // 2)):
        ref[...] = jnp.concatenate(
            [
                sums[d][:, at + j * count : at + (j + 1) * count]
                for j in range(bands // parts)
                for d in range(parts)
            ],
            axis=1,
        )

    @pl.loop(1, bands)
    def _(o):
        f_copy(o, False).wait_send()
        a_copy(o, False).wait_send()

    @pl.loop(0, bands)
    def _(slot):
        part_copy(part, across, slot, x_send).wait_send()
        part_copy(part, mate, slot, mate_send.at[0]).wait_send()
        part_copy(across, mate, slot, mate_send.at[1]).wait_send()

    @pl.loop(1, total_devices)
    def _(o):
        block_copy(o, False).wait_send()


def run_gram(f, a, bands, parts, total_cells):
    lanes, cells = f.shape[1:]
    count = lanes // (NY // YB)
    orb_count = count * parts
    wide = 2 * bands * count // parts
    whole = pl.BlockSpec(memory_space=pltpu.VMEM)
    out = jax.ShapeDtypeStruct((orb_count, bands * orb_count // parts), jnp.float32)
    dma = pltpu.SemaphoreType.DMA
    return pl.pallas_call(
        functools.partial(gram_kernel, bands, parts, total_cells),
        out_shape=(out, out),
        in_specs=[whole] * 2,
        out_specs=(whole, whole),
        scratch_shapes=[
            pltpu.VMEM((parts, bands, lanes, cells), jnp.bfloat16),
            pltpu.VMEM((bands, lanes, cells), jnp.bfloat16),
            pltpu.VMEM((bands, parts, orb_count, wide), jnp.float32),
            pltpu.VMEM((bands * parts, orb_count, wide), jnp.float32),
            dma((bands,)), dma((parts, bands)), dma((bands,)), dma((bands,)),
            dma((bands,)), dma((2, bands)), dma((2,)),
            dma((bands * parts,)), dma((bands * parts,)),
        ],
        compiler_params=pltpu.CompilerParams(
            collective_id=0, has_side_effects=True, vmem_limit_bytes=56 * 1024 * 1024
        ),
        name="gram",
    )(f, a)


def whole_orbitals(orbitals, boundary, potential):
    orb_count, planes_here, plane = orbitals.shape
    parts = lax.axis_size("domain")
    bands = lax.axis_size("band")
    part = lax.axis_index("domain")
    count = orb_count // parts

    split = orbitals.reshape(parts, count, planes_here, plane).transpose(0, 2, 1, 3)
    mine = lax.all_to_all(split, "domain", split_axis=0, concat_axis=0, tiled=True)
    mine = mine.reshape(parts * planes_here, count, plane)
    rim = lax.dynamic_slice_in_dim(boundary, part * count, count, 0).transpose(1, 0, 2)
    pot = lax.all_gather(potential, "domain", axis=0, tiled=True)
    f, a = run_filter(mine, rim, pot)

    return run_gram(f, a, bands, parts, parts * planes_here * plane)


def solution(mesh):
    parts, bands = mesh.shape["domain"], mesh.shape["band"]

    def body(orbitals, boundary, potential):
        fits = (
            orbitals.shape[0] * (NY // YB) == LANES * parts
            and orbitals.shape[1] * parts == bands
            and bands % parts == 0
            and parts == 4
        )
        return (whole_orbitals if fits else per_device)(orbitals, boundary, potential)

    return jax.shard_map(
        body,
        mesh=mesh,
        in_specs=(P("band", "domain", None), P("band", None, None), P("domain", None)),
        out_specs=(P("band", "domain"), P("band", "domain")),
        check_vma=False,
    )
```

```python
import functools

import jax
import jax.numpy as jnp
from jax import lax
from jax.experimental import pallas as pl
from jax.experimental.pallas import tpu as pltpu
from jax.sharding import PartitionSpec as P

NX = 160
NY = 32
NZ_DEV = 2
DEGREE = 4
LANES = 128
PAD = 8
YB = 8
GAP = 2
MESH = pl.DeviceIdType.MESH


filter_center = 5.5
filter_radius = 4.5


def padded_2(cells, sides, width):
    for axis, dim in sides:
        count = lax.axis_size(axis)
        ends = count - 1
        head = lax.slice_in_dim(cells, 0, width, axis=dim)
        tail = lax.slice_in_dim(cells, cells.shape[dim] - width, cells.shape[dim], axis=dim)
        cells = jnp.concatenate(
            [
                lax.ppermute(tail, axis, [(i, (i + 1) % count) for i in range(ends)]),
                cells,
                lax.ppermute(head, axis, [((i + 1) % count, i) for i in range(ends)]),
            ],
            axis=dim,
        )
    return cells


def second_diff(values, axis_pos):
    near = jnp.roll(values, 1, axis_pos) + jnp.roll(values, -1, axis_pos)
    far = jnp.roll(values, 2, axis_pos) + jnp.roll(values, -2, axis_pos)
    return (16.0 * near - far - 30.0 * values) / 12.0


def plane_part(values):
    shaped = values.reshape(values.shape[:-1] + (NY, NX))
    total = second_diff(shaped, -1) + second_diff(shaped, -2)
    return total.reshape(values.shape)


def hamiltonian(padded, potential):
    middle = padded[:, 2:-2]
    z_part = (
        16.0 * (padded[:, 1:-3] + padded[:, 3:-1])
        - (padded[:, :-4] + padded[:, 4:])
        - 30.0 * middle
    ) / 12.0
    laplace = z_part + plane_part(middle)
    return -0.5 * laplace + potential.astype(jnp.float32) * middle


def chebyshev(apply_ham, orb_block):
    earlier = orb_block
    current = (
        (apply_ham(orb_block) - filter_center * orb_block.astype(jnp.float32)) / filter_radius
    ).astype(jnp.bfloat16)
    for degree_step in range(DEGREE - 1):
        following = (
            2.0 * (apply_ham(current) - filter_center * current.astype(jnp.float32)) / filter_radius
        )
        following = (following - earlier.astype(jnp.float32)).astype(jnp.bfloat16)
        earlier, current = (current, following)
    return (current, apply_ham(current).astype(jnp.bfloat16))


def per_device(orbitals, boundary, potential):
    orb_count = orbitals.shape[0]
    domain_pos = lax.axis_index("domain")
    domain_count = lax.axis_size("domain")
    last_pos = domain_count - 1

    def apply_ham(values):
        padded = padded_2(values, (("domain", 1),), 2)
        lower_rim = jnp.where(domain_pos == 0, boundary[:, 0:2], padded[:, 0:2])
        upper_rim = jnp.where(domain_pos == last_pos, boundary[:, 2:4], padded[:, -2:])
        padded = jnp.concatenate([lower_rim, padded[:, 2:-2], upper_rim], axis=1).astype(
            jnp.float32
        )
        return hamiltonian(padded, potential)

    filtered, applied = chebyshev(apply_ham, orbitals)
    filtered = filtered.reshape(orb_count, -1)
    applied = applied.reshape(orb_count, -1)
    cell_y, cell_h = (
        lax.all_to_all(filtered, "band", split_axis=1, concat_axis=0, tiled=True),
        lax.all_to_all(applied, "band", split_axis=1, concat_axis=0, tiled=True),
    )
    cell_y, cell_h = (
        lax.all_gather(cell_y, "domain", axis=1, tiled=True),
        lax.all_gather(cell_h, "domain", axis=1, tiled=True),
    )
    column_count = cell_y.shape[0] // domain_count
    column_y = lax.dynamic_slice_in_dim(cell_y, domain_pos * column_count, column_count, 0)
    column_h = lax.dynamic_slice_in_dim(cell_h, domain_pos * column_count, column_count, 0)
    contract_dims = (((1,), (1,)), ((), ()))
    with_y = lax.dot_general(cell_y, column_y, contract_dims, preferred_element_type=jnp.float32)
    with_h = lax.dot_general(cell_y, column_h, contract_dims, preferred_element_type=jnp.float32)
    summed = lax.psum_scatter(
        jnp.concatenate([with_y, with_h], axis=1), "band", scatter_dimension=0, tiled=True
    )
    total_cells = NZ_DEV * NY * NX * domain_count
    correlation = summed[:, :column_count] / total_cells
    projected = summed[:, column_count:] / total_cells
    return (correlation, projected)


SCALE = 2.0 / filter_radius
K_NEAR = SCALE * 16.0 / 24.0
K_FAR = SCALE / 24.0


def plane_in(src):
    group = YB * NX
    rows = jnp.concatenate(
        [src[:, g * group : (g + 1) * group].astype(jnp.float32) for g in range(NY // YB)], axis=0
    )
    return rows.T.reshape(YB, NX, LANES)


def fill_rims(buf, z):
    for yi in range(YB):
        buf[z, yi + GAP, PAD - 2 : PAD] = buf[z, yi + GAP, PAD + NX - 2 : PAD + NX]
        buf[z, yi + GAP, PAD + NX : PAD + NX + 2] = buf[z, yi + GAP, PAD : PAD + 2]
    turn = LANES // (NY // YB)
    for k in range(GAP):
        low = buf[z, YB + k, PAD : PAD + NX]
        buf[z, k, PAD : PAD + NX] = pltpu.roll(low, turn, 1)
        high = buf[z, GAP + k, PAD : PAD + NX]
        buf[z, GAP + YB + k, PAD : PAD + NX] = pltpu.roll(high, LANES - turn, 1)


def apply_step(cur, out, coef, kind, planes):
    chunk = 40

    @pl.loop(0, YB)
    def _(yi):
        for x0 in range(PAD, PAD + NX, chunk):
            here = pl.ds(x0, chunk)
            mids = [cur[z, yi + GAP, here] for z in range(planes + 4)]
            for z in range(planes):
                zc = z + 2
                v = mids[zc]
                near = (
                    (mids[zc - 1] + mids[zc + 1])
                    + (cur[zc, yi + 1, here] + cur[zc, yi + 3, here])
                    + (cur[zc, yi + GAP, pl.ds(x0 - 1, chunk)] + cur[zc, yi + GAP, pl.ds(x0 + 1, chunk)])
                )
                far = (
                    (mids[zc - 2] + mids[zc + 2])
                    + (cur[zc, yi, here] + cur[zc, yi + 4, here])
                    + (cur[zc, yi + GAP, pl.ds(x0 - 2, chunk)] + cur[zc, yi + GAP, pl.ds(x0 + 2, chunk)])
                )
                r = coef[z, yi, pl.ds(x0 - PAD, chunk)] * v - K_NEAR * near + K_FAR * far
                if kind == "first":
                    r = 0.5 * r
                elif kind == "next":
                    r = r - out[zc, yi + GAP, here]
                else:
                    r = r * (1.0 / SCALE) + filter_center * v
                out[zc, yi + GAP, here] = r.astype(jnp.bfloat16).astype(jnp.float32)


def filter_kernel(orb_ref, rim_ref, pot_ref, f_ref, a_ref, buf_a, buf_b, coef):
    planes = orb_ref.shape[0]
    count = orb_ref.shape[1]

    for k in range(4):
        z = k if k < 2 else planes + k
        rim = plane_in(rim_ref[k])
        buf_a[z, GAP : GAP + YB, PAD : PAD + NX] = rim
        buf_b[z, GAP : GAP + YB, PAD : PAD + NX] = rim

    @pl.loop(0, planes)
    def _(z):
        row = pot_ref[z].astype(jnp.float32)
        spread = jnp.broadcast_to((row - 1.75) * SCALE, (count, row.shape[-1]))
        coef[z] = plane_in(spread)
        buf_a[z + 2, GAP : GAP + YB, PAD : PAD + NX] = plane_in(orb_ref[z])
        fill_rims(buf_a, z + 2)

    def rims(buf):
        @pl.loop(0, planes)
        def _(z):
            fill_rims(buf, z + 2)

    def emit(buf, ref):
        @pl.loop(0, planes)
        def _(z):
            cells = buf[z + 2, GAP : GAP + YB, PAD : PAD + NX].reshape(YB * NX, LANES)
            ref[z] = cells.T.astype(jnp.bfloat16)

    cur, other = buf_a, buf_b
    apply_step(cur, other, coef, "first", planes)
    for _ in range(DEGREE - 1):
        cur, other = other, cur
        rims(cur)
        apply_step(cur, other, coef, "next", planes)
    cur, other = other, cur
    rims(cur)
    emit(cur, f_ref)
    apply_step(cur, other, coef, "last", planes)
    emit(other, a_ref)


def run_filter(orb, rim, pot):
    planes = orb.shape[0]
    out = jax.ShapeDtypeStruct((planes, LANES, YB * NX), jnp.bfloat16)
    whole = pl.BlockSpec(memory_space=pltpu.VMEM)
    field = pltpu.VMEM((planes + 4, YB + 2 * GAP, NX + 2 * PAD, LANES), jnp.float32)
    return pl.pallas_call(
        filter_kernel,
        out_shape=(out, out),
        in_specs=[whole] * 3,
        out_specs=(whole, whole),
        scratch_shapes=[field, field, pltpu.VMEM((planes, YB, NX, LANES), jnp.float32)],
        compiler_params=pltpu.CompilerParams(vmem_limit_bytes=56 * 1024 * 1024),
        name="chebyshev",
    )(orb, rim, pot[:, None])


def meet_all(bands, parts, band, part):
    barrier = pltpu.get_barrier_semaphore()
    total = bands * parts
    me = band * parts + part

    @pl.loop(1, total)
    def _(o):
        t = lax.rem(me + o, total)
        pl.semaphore_signal(
            barrier, inc=1, device_id=(t // parts, lax.rem(t, parts)), device_id_type=MESH
        )

    pl.semaphore_wait(barrier, total - 1)


def gram_kernel(
    bands, parts, total_cells,
    f_ref, a_ref, c_ref, p_ref,
    all_f, own_a, blocks, landed,
    f_send, f_recv, a_send, a_recv, x_send, mate_send, local_sem, b_send, b_recv,
):
    band, part = lax.axis_index("band"), lax.axis_index("domain")
    lanes, cells = f_ref.shape[1:]
    count = blocks.shape[2] // parts
    groups = lanes // count
    rows = bands * count
    wide = 2 * rows // parts
    mate = part + 1 - 2 * lax.rem(part, 2)
    across = lax.rem(part + 2, parts)
    across_mate = lax.rem(mate + 2, parts)
    meet_all(bands, parts, band, part)

    core = lax.rem(part, 2)

    def turned(o, total):
        return o + core * (total - 2 * o)

    def band_copy(src, dst, send, recv, o, incoming, rows_at=slice(None)):
        o = turned(o, bands)
        peer = lax.rem(band + o, bands)
        source = lax.rem(band - o + bands, bands)
        slot = source if incoming else band
        return pltpu.make_async_remote_copy(
            src_ref=src.at[peer, rows_at], dst_ref=dst.at[slot, rows_at], send_sem=send.at[o],
            recv_sem=recv.at[slot], device_id=(peer, part), device_id_type=MESH,
        )

    def f_copy(o, incoming, rows_at=slice(None)):
        return band_copy(f_ref, all_f.at[part], f_send, f_recv.at[part], o, incoming, rows_at)

    def a_copy(o, incoming, rows_at=slice(None)):
        return band_copy(a_ref, own_a, a_send, a_recv, o, incoming, rows_at)

    def start_piece(copy, k):
        g, o = k // (bands - 1), 1 + lax.rem(k, bands - 1)
        copy(o, False, pl.ds(pl.multiple_of(g * count, count), count)).start()

    def from_band(o):
        return lax.rem(band - turned(o, bands) + bands, bands)

    def part_copy(owner, to, slot, send):
        return pltpu.make_async_remote_copy(
            src_ref=all_f.at[owner, slot], dst_ref=all_f.at[owner, slot], send_sem=send.at[slot],
            recv_sem=f_recv.at[owner, slot], device_id=(band, to), device_id_type=MESH,
        )

    keep_f = pltpu.make_async_copy(f_ref.at[band], all_f.at[part, band], local_sem.at[0])
    keep_a = pltpu.make_async_copy(a_ref.at[band], own_a.at[band], local_sem.at[1])
    keep_f.start()
    keep_a.start()

    @pl.loop(0, groups * (bands - 1))
    def _(k):
        start_piece(f_copy, k)

    keep_f.wait()
    part_copy(part, across, band, x_send).start()
    part_copy(part, mate, band, mate_send.at[0]).start()

    @pl.loop(1, bands)
    def _(o):
        slot = from_band(o)
        f_copy(o, True).wait_recv()
        part_copy(part, across, slot, x_send).start()
        part_copy(part, mate, slot, mate_send.at[0]).start()
        for i in range(groups):
            start_piece(a_copy, (o - 1) * groups + i)

    @pl.loop(0, bands)
    def _(o):
        slot = lax.rem(from_band(o) + bands, bands)
        part_copy(across, mate, slot, mate_send.at[1]).wait_recv()
        part_copy(across, mate, slot, mate_send.at[1]).start()

    keep_a.wait()

    @pl.loop(1, bands)
    def _(o):
        a_copy(o, True).wait_recv()

    def add_rows(owner):
        total = jnp.zeros((rows, 2 * rows), jnp.float32)
        for g in range(groups):
            at = slice(g * count, (g + 1) * count)
            sides = []
            for k in range(parts):
                two = slice(k * bands // parts, (k + 1) * bands // parts)
                sides.append(all_f[part, two, at].reshape(wide // 2, cells))
                sides.append(own_a[two, at].reshape(wide // 2, cells))
            total += lax.dot_general(
                all_f[owner, :, at].reshape(rows, cells),
                jnp.concatenate(sides, axis=0),
                (((1,), (1,)), ((), ())),
                preferred_element_type=jnp.float32,
            )
        for k in range(parts):
            blocks[:, k, pl.ds(pl.multiple_of(owner * count, count), count)] = total[
                :, k * wide : (k + 1) * wide
            ].reshape(bands, count, wide)

    @pl.loop(0, bands)
    def _(slot):
        part_copy(mate, part, slot, mate_send.at[0]).wait_recv()
        part_copy(across_mate, part, slot, mate_send.at[1]).wait_recv()

    @pl.loop(0, parts)
    def _(k):
        add_rows(k)

    me = band * parts + part
    total_devices = bands * parts

    def block_copy(o, incoming):
        o = turned(o, total_devices)
        t = lax.rem(me + o, total_devices)
        source = lax.rem(me - o + total_devices, total_devices)
        slot = source if incoming else me
        return pltpu.make_async_remote_copy(
            src_ref=blocks.at[t // parts, lax.rem(t, parts)], dst_ref=landed.at[slot],
            send_sem=b_send.at[o], recv_sem=b_recv.at[slot],
            device_id=(t // parts, lax.rem(t, parts)), device_id_type=MESH,
        )

    @pl.loop(1, total_devices)
    def _(o):
        block_copy(o, False).start()

    keep = pltpu.make_async_copy(blocks.at[band, part], landed.at[me], local_sem.at[0])
    keep.start()
    keep.wait()

    @pl.loop(1, total_devices)
    def _(o):
        block_copy(o, True).wait_recv()

    sums = []
    for d in range(parts):
        total = landed[d]
        for b in range(1, bands):
            total = total + landed[b * parts + d]
        sums.append(total * (1.0 / total_cells))
    for ref, at in ((c_ref, 0), (p_ref, wide // 2)):
        ref[...] = jnp.concatenate(
            [
                sums[d][:, at + j * count : at + (j + 1) * count]
                for j in range(bands // parts)
                for d in range(parts)
            ],
            axis=1,
        )

    @pl.loop(1, bands)
    def _(o):
        f_copy(o, False).wait_send()
        a_copy(o, False).wait_send()

    @pl.loop(0, bands)
    def _(slot):
        part_copy(part, across, slot, x_send).wait_send()
        part_copy(part, mate, slot, mate_send.at[0]).wait_send()
        part_copy(across, mate, slot, mate_send.at[1]).wait_send()

    @pl.loop(1, total_devices)
    def _(o):
        block_copy(o, False).wait_send()


def run_gram(f, a, bands, parts, total_cells):
    lanes, cells = f.shape[1:]
    count = lanes // (NY // YB)
    orb_count = count * parts
    wide = 2 * bands * count // parts
    whole = pl.BlockSpec(memory_space=pltpu.VMEM)
    out = jax.ShapeDtypeStruct((orb_count, bands * orb_count // parts), jnp.float32)
    dma = pltpu.SemaphoreType.DMA
    return pl.pallas_call(
        functools.partial(gram_kernel, bands, parts, total_cells),
        out_shape=(out, out),
        in_specs=[whole] * 2,
        out_specs=(whole, whole),
        scratch_shapes=[
            pltpu.VMEM((parts, bands, lanes, cells), jnp.bfloat16),
            pltpu.VMEM((bands, lanes, cells), jnp.bfloat16),
            pltpu.VMEM((bands, parts, orb_count, wide), jnp.float32),
            pltpu.VMEM((bands * parts, orb_count, wide), jnp.float32),
            dma((bands,)), dma((parts, bands)), dma((bands,)), dma((bands,)),
            dma((bands,)), dma((2, bands)), dma((2,)),
            dma((bands * parts,)), dma((bands * parts,)),
        ],
        compiler_params=pltpu.CompilerParams(
            collective_id=0, has_side_effects=True, vmem_limit_bytes=56 * 1024 * 1024
        ),
        name="gram",
    )(f, a)


def whole_orbitals(orbitals, boundary, potential):
    orb_count, planes_here, plane = orbitals.shape
    parts = lax.axis_size("domain")
    bands = lax.axis_size("band")
    part = lax.axis_index("domain")
    count = orb_count // parts

    split = orbitals.reshape(parts, count, planes_here, plane).transpose(0, 2, 1, 3)
    mine = lax.all_to_all(split, "domain", split_axis=0, concat_axis=0, tiled=True)
    mine = mine.reshape(parts * planes_here, count, plane)
    rim = lax.dynamic_slice_in_dim(boundary, part * count, count, 0).transpose(1, 0, 2)
    pot = lax.all_gather(potential, "domain", axis=0, tiled=True)
    f, a = run_filter(mine, rim, pot)

    return run_gram(f, a, bands, parts, parts * planes_here * plane)


def solution(mesh):
    parts, bands = mesh.shape["domain"], mesh.shape["band"]

    def body(orbitals, boundary, potential):
        fits = (
            orbitals.shape[0] * (NY // YB) == LANES * parts
            and orbitals.shape[1] * parts == bands
            and bands % parts == 0
            and parts == 4
        )
        return (whole_orbitals if fits else per_device)(orbitals, boundary, potential)

    return jax.shard_map(
        body,
        mesh=mesh,
        in_specs=(P("band", "domain", None), P("band", None, None), P("domain", None)),
        out_specs=(P("band", "domain"), P("band", "domain")),
        check_vma=False,
    )
```

```python
import functools

import jax
import jax.numpy as jnp
from jax import lax
from jax.experimental import pallas as pl
from jax.experimental.pallas import tpu as pltpu
from jax.sharding import PartitionSpec as P

NX = 160
NY = 32
NZ_DEV = 2
DEGREE = 4
LANES = 128
PAD = 8
YB = 8
GAP = 2
MESH = pl.DeviceIdType.MESH


filter_center = 5.5
filter_radius = 4.5


def padded_2(cells, sides, width):
    for axis, dim in sides:
        count = lax.axis_size(axis)
        ends = count - 1
        head = lax.slice_in_dim(cells, 0, width, axis=dim)
        tail = lax.slice_in_dim(cells, cells.shape[dim] - width, cells.shape[dim], axis=dim)
        cells = jnp.concatenate(
            [
                lax.ppermute(tail, axis, [(i, (i + 1) % count) for i in range(ends)]),
                cells,
                lax.ppermute(head, axis, [((i + 1) % count, i) for i in range(ends)]),
            ],
            axis=dim,
        )
    return cells


def second_diff(values, axis_pos):
    near = jnp.roll(values, 1, axis_pos) + jnp.roll(values, -1, axis_pos)
    far = jnp.roll(values, 2, axis_pos) + jnp.roll(values, -2, axis_pos)
    return (16.0 * near - far - 30.0 * values) / 12.0


def plane_part(values):
    shaped = values.reshape(values.shape[:-1] + (NY, NX))
    total = second_diff(shaped, -1) + second_diff(shaped, -2)
    return total.reshape(values.shape)


def hamiltonian(padded, potential):
    middle = padded[:, 2:-2]
    z_part = (
        16.0 * (padded[:, 1:-3] + padded[:, 3:-1])
        - (padded[:, :-4] + padded[:, 4:])
        - 30.0 * middle
    ) / 12.0
    laplace = z_part + plane_part(middle)
    return -0.5 * laplace + potential.astype(jnp.float32) * middle


def chebyshev(apply_ham, orb_block):
    earlier = orb_block
    current = (
        (apply_ham(orb_block) - filter_center * orb_block.astype(jnp.float32)) / filter_radius
    ).astype(jnp.bfloat16)
    for degree_step in range(DEGREE - 1):
        following = (
            2.0 * (apply_ham(current) - filter_center * current.astype(jnp.float32)) / filter_radius
        )
        following = (following - earlier.astype(jnp.float32)).astype(jnp.bfloat16)
        earlier, current = (current, following)
    return (current, apply_ham(current).astype(jnp.bfloat16))


def per_device(orbitals, boundary, potential):
    orb_count = orbitals.shape[0]
    domain_pos = lax.axis_index("domain")
    domain_count = lax.axis_size("domain")
    last_pos = domain_count - 1

    def apply_ham(values):
        padded = padded_2(values, (("domain", 1),), 2)
        lower_rim = jnp.where(domain_pos == 0, boundary[:, 0:2], padded[:, 0:2])
        upper_rim = jnp.where(domain_pos == last_pos, boundary[:, 2:4], padded[:, -2:])
        padded = jnp.concatenate([lower_rim, padded[:, 2:-2], upper_rim], axis=1).astype(
            jnp.float32
        )
        return hamiltonian(padded, potential)

    filtered, applied = chebyshev(apply_ham, orbitals)
    filtered = filtered.reshape(orb_count, -1)
    applied = applied.reshape(orb_count, -1)
    cell_y, cell_h = (
        lax.all_to_all(filtered, "band", split_axis=1, concat_axis=0, tiled=True),
        lax.all_to_all(applied, "band", split_axis=1, concat_axis=0, tiled=True),
    )
    cell_y, cell_h = (
        lax.all_gather(cell_y, "domain", axis=1, tiled=True),
        lax.all_gather(cell_h, "domain", axis=1, tiled=True),
    )
    column_count = cell_y.shape[0] // domain_count
    column_y = lax.dynamic_slice_in_dim(cell_y, domain_pos * column_count, column_count, 0)
    column_h = lax.dynamic_slice_in_dim(cell_h, domain_pos * column_count, column_count, 0)
    contract_dims = (((1,), (1,)), ((), ()))
    with_y = lax.dot_general(cell_y, column_y, contract_dims, preferred_element_type=jnp.float32)
    with_h = lax.dot_general(cell_y, column_h, contract_dims, preferred_element_type=jnp.float32)
    summed = lax.psum_scatter(
        jnp.concatenate([with_y, with_h], axis=1), "band", scatter_dimension=0, tiled=True
    )
    total_cells = NZ_DEV * NY * NX * domain_count
    correlation = summed[:, :column_count] / total_cells
    projected = summed[:, column_count:] / total_cells
    return (correlation, projected)


SCALE = 2.0 / filter_radius
K_NEAR = SCALE * 16.0 / 24.0
K_FAR = SCALE / 24.0


def plane_in(src):
    group = YB * NX
    rows = jnp.concatenate(
        [src[:, g * group : (g + 1) * group].astype(jnp.float32) for g in range(NY // YB)], axis=0
    )
    return rows.T.reshape(YB, NX, LANES)


def fill_rims(buf, z):
    for yi in range(YB):
        buf[z, yi + GAP, PAD - 2 : PAD] = buf[z, yi + GAP, PAD + NX - 2 : PAD + NX]
        buf[z, yi + GAP, PAD + NX : PAD + NX + 2] = buf[z, yi + GAP, PAD : PAD + 2]
    turn = LANES // (NY // YB)
    for k in range(GAP):
        low = buf[z, YB + k, PAD : PAD + NX]
        buf[z, k, PAD : PAD + NX] = pltpu.roll(low, turn, 1)
        high = buf[z, GAP + k, PAD : PAD + NX]
        buf[z, GAP + YB + k, PAD : PAD + NX] = pltpu.roll(high, LANES - turn, 1)


def apply_step(cur, out, coef, kind, planes):
    chunk = 40

    @pl.loop(0, YB)
    def _(yi):
        for x0 in range(PAD, PAD + NX, chunk):
            here = pl.ds(x0, chunk)
            mids = [cur[z, yi + GAP, here] for z in range(planes + 4)]
            for z in range(planes):
                zc = z + 2
                v = mids[zc]
                near = (
                    (mids[zc - 1] + mids[zc + 1])
                    + (cur[zc, yi + 1, here] + cur[zc, yi + 3, here])
                    + (cur[zc, yi + GAP, pl.ds(x0 - 1, chunk)] + cur[zc, yi + GAP, pl.ds(x0 + 1, chunk)])
                )
                far = (
                    (mids[zc - 2] + mids[zc + 2])
                    + (cur[zc, yi, here] + cur[zc, yi + 4, here])
                    + (cur[zc, yi + GAP, pl.ds(x0 - 2, chunk)] + cur[zc, yi + GAP, pl.ds(x0 + 2, chunk)])
                )
                r = coef[z, yi, pl.ds(x0 - PAD, chunk)] * v - K_NEAR * near + K_FAR * far
                if kind == "first":
                    r = 0.5 * r
                elif kind == "next":
                    r = r - out[zc, yi + GAP, here]
                else:
                    r = r * (1.0 / SCALE) + filter_center * v
                out[zc, yi + GAP, here] = r.astype(jnp.bfloat16).astype(jnp.float32)


def filter_kernel(orb_ref, rim_ref, pot_ref, f_ref, a_ref, buf_a, buf_b, coef):
    planes = orb_ref.shape[0]
    count = orb_ref.shape[1]

    for k in range(4):
        z = k if k < 2 else planes + k
        rim = plane_in(rim_ref[k])
        buf_a[z, GAP : GAP + YB, PAD : PAD + NX] = rim
        buf_b[z, GAP : GAP + YB, PAD : PAD + NX] = rim

    @pl.loop(0, planes)
    def _(z):
        row = pot_ref[z].astype(jnp.float32)
        spread = jnp.broadcast_to((row - 1.75) * SCALE, (count, row.shape[-1]))
        coef[z] = plane_in(spread)
        buf_a[z + 2, GAP : GAP + YB, PAD : PAD + NX] = plane_in(orb_ref[z])
        fill_rims(buf_a, z + 2)

    def rims(buf):
        @pl.loop(0, planes)
        def _(z):
            fill_rims(buf, z + 2)

    def emit(buf, ref):
        @pl.loop(0, planes)
        def _(z):
            cells = buf[z + 2, GAP : GAP + YB, PAD : PAD + NX].reshape(YB * NX, LANES)
            ref[z] = cells.T.astype(jnp.bfloat16)

    cur, other = buf_a, buf_b
    apply_step(cur, other, coef, "first", planes)
    for _ in range(DEGREE - 1):
        cur, other = other, cur
        rims(cur)
        apply_step(cur, other, coef, "next", planes)
    cur, other = other, cur
    rims(cur)
    emit(cur, f_ref)
    apply_step(cur, other, coef, "last", planes)
    emit(other, a_ref)


def run_filter(orb, rim, pot):
    planes = orb.shape[0]
    out = jax.ShapeDtypeStruct((planes, LANES, YB * NX), jnp.bfloat16)
    whole = pl.BlockSpec(memory_space=pltpu.VMEM)
    field = pltpu.VMEM((planes + 4, YB + 2 * GAP, NX + 2 * PAD, LANES), jnp.float32)
    return pl.pallas_call(
        filter_kernel,
        out_shape=(out, out),
        in_specs=[whole] * 3,
        out_specs=(whole, whole),
        scratch_shapes=[field, field, pltpu.VMEM((planes, YB, NX, LANES), jnp.float32)],
        compiler_params=pltpu.CompilerParams(vmem_limit_bytes=56 * 1024 * 1024),
        name="chebyshev",
    )(orb, rim, pot[:, None])


def meet_all(bands, parts, band, part):
    barrier = pltpu.get_barrier_semaphore()
    total = bands * parts
    me = band * parts + part

    @pl.loop(1, total)
    def _(o):
        t = lax.rem(me + o, total)
        pl.semaphore_signal(
            barrier, inc=1, device_id=(t // parts, lax.rem(t, parts)), device_id_type=MESH
        )

    pl.semaphore_wait(barrier, total - 1)


def gram_kernel(
    bands, parts, total_cells,
    f_ref, a_ref, c_ref, p_ref,
    all_f, own_a, blocks, landed,
    f_send, f_recv, a_send, a_recv, x_send, mate_send, local_sem, b_send, b_recv,
):
    band, part = lax.axis_index("band"), lax.axis_index("domain")
    lanes, cells = f_ref.shape[1:]
    groups = NY // YB
    count = lanes // groups
    rows = bands * count
    wide = rows // parts
    mate = part + 1 - 2 * lax.rem(part, 2)
    across = lax.rem(part + 2, parts)
    across_mate = lax.rem(mate + 2, parts)
    meet_all(bands, parts, band, part)

    core = lax.rem(part, 2)

    def turned(o, total):
        return o + core * (total - 2 * o)

    def band_copy(src, dst, send, recv, o, incoming, rows_at=slice(None)):
        o = turned(o, bands)
        peer = lax.rem(band + o, bands)
        source = lax.rem(band - o + bands, bands)
        slot = source if incoming else band
        return pltpu.make_async_remote_copy(
            src_ref=src.at[peer, rows_at], dst_ref=dst.at[slot, rows_at], send_sem=send.at[o],
            recv_sem=recv.at[slot], device_id=(peer, part), device_id_type=MESH,
        )

    def f_copy(o, incoming, rows_at=slice(None)):
        return band_copy(f_ref, all_f.at[part], f_send, f_recv.at[part], o, incoming, rows_at)

    def a_copy(o, incoming, rows_at=slice(None)):
        return band_copy(a_ref, own_a, a_send, a_recv, o, incoming, rows_at)

    def start_piece(copy, k):
        g, o = k // (bands - 1), 1 + lax.rem(k, bands - 1)
        copy(o, False, pl.ds(pl.multiple_of(g * count, count), count)).start()

    def from_band(o):
        return lax.rem(band - turned(o, bands) + bands, bands)

    def part_copy(owner, to, slot, send):
        return pltpu.make_async_remote_copy(
            src_ref=all_f.at[owner, slot], dst_ref=all_f.at[owner, slot], send_sem=send.at[slot],
            recv_sem=f_recv.at[owner, slot], device_id=(band, to), device_id_type=MESH,
        )

    keep_f = pltpu.make_async_copy(f_ref.at[band], all_f.at[part, band], local_sem.at[0])
    keep_a = pltpu.make_async_copy(a_ref.at[band], own_a.at[band], local_sem.at[1])
    keep_f.start()
    keep_a.start()

    @pl.loop(0, groups * (bands - 1))
    def _(k):
        start_piece(f_copy, k)

    keep_f.wait()
    part_copy(part, across, band, x_send).start()
    part_copy(part, mate, band, mate_send.at[0]).start()

    @pl.loop(1, bands)
    def _(o):
        slot = from_band(o)
        f_copy(o, True).wait_recv()
        part_copy(part, across, slot, x_send).start()
        part_copy(part, mate, slot, mate_send.at[0]).start()
        for i in range(groups):
            start_piece(a_copy, (o - 1) * groups + i)

    @pl.loop(0, bands)
    def _(o):
        slot = lax.rem(from_band(o) + bands, bands)
        part_copy(across, mate, slot, mate_send.at[1]).wait_recv()
        part_copy(across, mate, slot, mate_send.at[1]).start()

    @pl.loop(0, bands)
    def _(slot):
        part_copy(mate, part, slot, mate_send.at[0]).wait_recv()
        part_copy(across_mate, part, slot, mate_send.at[1]).wait_recv()

    me = band * parts + part
    total_devices = bands * parts

    def block_copy(m, o, incoming, rows_at=slice(None)):
        o = turned(o, total_devices)
        t = lax.rem(me + o, total_devices)
        source = lax.rem(me - o + total_devices, total_devices)
        slot = source if incoming else me
        return pltpu.make_async_remote_copy(
            src_ref=blocks.at[m, t // parts, lax.rem(t, parts), rows_at],
            dst_ref=landed.at[m, slot, rows_at],
            send_sem=b_send.at[m, o], recv_sem=b_recv.at[m, slot],
            device_id=(t // parts, lax.rem(t, parts)), device_id_type=MESH,
        )

    def product(owner, columns):
        total = jnp.zeros((rows, rows), jnp.float32)
        for g in range(groups):
            at = slice(g * count, (g + 1) * count)
            total += lax.dot_general(
                all_f[owner, :, at].reshape(rows, cells),
                columns[:, at].reshape(rows, cells),
                (((1,), (1,)), ((), ())),
                preferred_element_type=jnp.float32,
            )
        return total

    def send_products(m, columns):
        @pl.loop(0, parts // 2)
        def _(p):
            pair = [product(2 * p + h, columns) for h in range(2)]
            at = pl.ds(pl.multiple_of(p * count, count), count)
            for k in range(parts):
                blocks[m, :, k, at] = jnp.concatenate(
                    [t[:, k * wide : (k + 1) * wide] for t in pair], axis=1
                ).reshape(bands, count, 2 * wide)

            @pl.loop(1, total_devices)
            def _(o):
                block_copy(m, o, False, at).start()

        keep = pltpu.make_async_copy(
            blocks.at[m, band, part], landed.at[m, me], local_sem.at[0]
        )
        keep.start()
        keep.wait()

    def finish(m, ref):
        @pl.loop(1, total_devices)
        def _(o):
            block_copy(m, o, True).wait_recv()

        sums = []
        for d in range(parts):
            total = landed[m, d]
            for b in range(1, bands):
                total = total + landed[m, b * parts + d]
            sums.append(total * (1.0 / total_cells))
        for k in range(parts):
            p, h = k // 2, k % 2
            ref[k * count : (k + 1) * count] = jnp.concatenate(
                [
                    sums[d][p * count : (p + 1) * count, h * wide + j * count : h * wide + (j + 1) * count]
                    for j in range(bands // parts)
                    for d in range(parts)
                ],
                axis=1,
            )

    send_products(0, all_f.at[part])
    keep_a.wait()

    @pl.loop(1, bands)
    def _(o):
        a_copy(o, True).wait_recv()

    send_products(1, own_a)
    finish(0, c_ref)
    finish(1, p_ref)

    @pl.loop(1, bands)
    def _(o):
        f_copy(o, False).wait_send()
        a_copy(o, False).wait_send()

    @pl.loop(0, bands)
    def _(slot):
        part_copy(part, across, slot, x_send).wait_send()
        part_copy(part, mate, slot, mate_send.at[0]).wait_send()
        part_copy(across, mate, slot, mate_send.at[1]).wait_send()

    @pl.loop(1, total_devices)
    def _(o):
        block_copy(0, o, False).wait_send()
        block_copy(1, o, False).wait_send()


def run_gram(f, a, bands, parts, total_cells):
    lanes, cells = f.shape[1:]
    count = lanes // (NY // YB)
    orb_count = count * parts
    block = (orb_count // 2, 2 * bands * count // parts)
    whole = pl.BlockSpec(memory_space=pltpu.VMEM)
    out = jax.ShapeDtypeStruct((orb_count, bands * orb_count // parts), jnp.float32)
    dma = pltpu.SemaphoreType.DMA
    return pl.pallas_call(
        functools.partial(gram_kernel, bands, parts, total_cells),
        out_shape=(out, out),
        in_specs=[whole] * 2,
        out_specs=(whole, whole),
        scratch_shapes=[
            pltpu.VMEM((parts, bands, lanes, cells), jnp.bfloat16),
            pltpu.VMEM((bands, lanes, cells), jnp.bfloat16),
            pltpu.VMEM((2, bands, parts, *block), jnp.float32),
            pltpu.VMEM((2, bands * parts, *block), jnp.float32),
            dma((bands,)), dma((parts, bands)), dma((bands,)), dma((bands,)),
            dma((bands,)), dma((2, bands)), dma((2,)),
            dma((2, bands * parts)), dma((2, bands * parts)),
        ],
        compiler_params=pltpu.CompilerParams(
            collective_id=0, has_side_effects=True, vmem_limit_bytes=56 * 1024 * 1024
        ),
        name="gram",
    )(f, a)


def whole_orbitals(orbitals, boundary, potential):
    orb_count, planes_here, plane = orbitals.shape
    parts = lax.axis_size("domain")
    bands = lax.axis_size("band")
    part = lax.axis_index("domain")
    count = orb_count // parts

    split = orbitals.reshape(parts, count, planes_here, plane).transpose(0, 2, 1, 3)
    mine = lax.all_to_all(split, "domain", split_axis=0, concat_axis=0, tiled=True)
    mine = mine.reshape(parts * planes_here, count, plane)
    rim = lax.dynamic_slice_in_dim(boundary, part * count, count, 0).transpose(1, 0, 2)
    rim, potential = lax.optimization_barrier((rim, potential))
    pot = lax.all_gather(potential, "domain", axis=0, tiled=True)
    f, a = run_filter(mine, rim, pot)

    return run_gram(f, a, bands, parts, parts * planes_here * plane)


def solution(mesh):
    parts, bands = mesh.shape["domain"], mesh.shape["band"]

    def body(orbitals, boundary, potential):
        fits = (
            orbitals.shape[0] * (NY // YB) == LANES * parts
            and orbitals.shape[1] * parts == bands
            and bands % parts == 0
            and parts == 4
        )
        return (whole_orbitals if fits else per_device)(orbitals, boundary, potential)

    return jax.shard_map(
        body,
        mesh=mesh,
        in_specs=(P("band", "domain", None), P("band", None, None), P("domain", None)),
        out_specs=(P("band", "domain"), P("band", "domain")),
        check_vma=False,
    )
```

```python
import functools

import jax
import jax.numpy as jnp
from jax import lax
from jax.experimental import pallas as pl
from jax.experimental.pallas import tpu as pltpu
from jax.sharding import PartitionSpec as P

NX = 160
NY = 32
NZ_DEV = 2
DEGREE = 4
LANES = 128
PAD = 8
YB = 8
GAP = 2
MESH = pl.DeviceIdType.MESH


filter_center = 5.5
filter_radius = 4.5


def padded_2(cells, sides, width):
    for axis, dim in sides:
        count = lax.axis_size(axis)
        ends = count - 1
        head = lax.slice_in_dim(cells, 0, width, axis=dim)
        tail = lax.slice_in_dim(cells, cells.shape[dim] - width, cells.shape[dim], axis=dim)
        cells = jnp.concatenate(
            [
                lax.ppermute(tail, axis, [(i, (i + 1) % count) for i in range(ends)]),
                cells,
                lax.ppermute(head, axis, [((i + 1) % count, i) for i in range(ends)]),
            ],
            axis=dim,
        )
    return cells


def second_diff(values, axis_pos):
    near = jnp.roll(values, 1, axis_pos) + jnp.roll(values, -1, axis_pos)
    far = jnp.roll(values, 2, axis_pos) + jnp.roll(values, -2, axis_pos)
    return (16.0 * near - far - 30.0 * values) / 12.0


def plane_part(values):
    shaped = values.reshape(values.shape[:-1] + (NY, NX))
    total = second_diff(shaped, -1) + second_diff(shaped, -2)
    return total.reshape(values.shape)


def hamiltonian(padded, potential):
    middle = padded[:, 2:-2]
    z_part = (
        16.0 * (padded[:, 1:-3] + padded[:, 3:-1])
        - (padded[:, :-4] + padded[:, 4:])
        - 30.0 * middle
    ) / 12.0
    laplace = z_part + plane_part(middle)
    return -0.5 * laplace + potential.astype(jnp.float32) * middle


def chebyshev(apply_ham, orb_block):
    earlier = orb_block
    current = (
        (apply_ham(orb_block) - filter_center * orb_block.astype(jnp.float32)) / filter_radius
    ).astype(jnp.bfloat16)
    for degree_step in range(DEGREE - 1):
        following = (
            2.0 * (apply_ham(current) - filter_center * current.astype(jnp.float32)) / filter_radius
        )
        following = (following - earlier.astype(jnp.float32)).astype(jnp.bfloat16)
        earlier, current = (current, following)
    return (current, apply_ham(current).astype(jnp.bfloat16))


def per_device(orbitals, boundary, potential):
    orb_count = orbitals.shape[0]
    domain_pos = lax.axis_index("domain")
    domain_count = lax.axis_size("domain")
    last_pos = domain_count - 1

    def apply_ham(values):
        padded = padded_2(values, (("domain", 1),), 2)
        lower_rim = jnp.where(domain_pos == 0, boundary[:, 0:2], padded[:, 0:2])
        upper_rim = jnp.where(domain_pos == last_pos, boundary[:, 2:4], padded[:, -2:])
        padded = jnp.concatenate([lower_rim, padded[:, 2:-2], upper_rim], axis=1).astype(
            jnp.float32
        )
        return hamiltonian(padded, potential)

    filtered, applied = chebyshev(apply_ham, orbitals)
    filtered = filtered.reshape(orb_count, -1)
    applied = applied.reshape(orb_count, -1)
    cell_y, cell_h = (
        lax.all_to_all(filtered, "band", split_axis=1, concat_axis=0, tiled=True),
        lax.all_to_all(applied, "band", split_axis=1, concat_axis=0, tiled=True),
    )
    cell_y, cell_h = (
        lax.all_gather(cell_y, "domain", axis=1, tiled=True),
        lax.all_gather(cell_h, "domain", axis=1, tiled=True),
    )
    column_count = cell_y.shape[0] // domain_count
    column_y = lax.dynamic_slice_in_dim(cell_y, domain_pos * column_count, column_count, 0)
    column_h = lax.dynamic_slice_in_dim(cell_h, domain_pos * column_count, column_count, 0)
    contract_dims = (((1,), (1,)), ((), ()))
    with_y = lax.dot_general(cell_y, column_y, contract_dims, preferred_element_type=jnp.float32)
    with_h = lax.dot_general(cell_y, column_h, contract_dims, preferred_element_type=jnp.float32)
    summed = lax.psum_scatter(
        jnp.concatenate([with_y, with_h], axis=1), "band", scatter_dimension=0, tiled=True
    )
    total_cells = NZ_DEV * NY * NX * domain_count
    correlation = summed[:, :column_count] / total_cells
    projected = summed[:, column_count:] / total_cells
    return (correlation, projected)


SCALE = 2.0 / filter_radius
K_NEAR = SCALE * 16.0 / 24.0
K_FAR = SCALE / 24.0


def plane_in(src):
    group = YB * NX
    rows = jnp.concatenate(
        [src[:, g * group : (g + 1) * group].astype(jnp.float32) for g in range(NY // YB)], axis=0
    )
    return rows.T.reshape(YB, NX, LANES)


def fill_rims(buf, z):
    for yi in range(YB):
        buf[z, yi + GAP, PAD - 2 : PAD] = buf[z, yi + GAP, PAD + NX - 2 : PAD + NX]
        buf[z, yi + GAP, PAD + NX : PAD + NX + 2] = buf[z, yi + GAP, PAD : PAD + 2]
    turn = LANES // (NY // YB)
    for k in range(GAP):
        low = buf[z, YB + k, PAD : PAD + NX]
        buf[z, k, PAD : PAD + NX] = pltpu.roll(low, turn, 1)
        high = buf[z, GAP + k, PAD : PAD + NX]
        buf[z, GAP + YB + k, PAD : PAD + NX] = pltpu.roll(high, LANES - turn, 1)


def apply_step(cur, out, coef, kind, planes):
    chunk = 40

    @pl.loop(0, YB)
    def _(yi):
        for x0 in range(PAD, PAD + NX, chunk):
            here = pl.ds(x0, chunk)
            mids = [cur[z, yi + GAP, here] for z in range(planes + 4)]
            for z in range(planes):
                zc = z + 2
                v = mids[zc]
                near = (
                    (mids[zc - 1] + mids[zc + 1])
                    + (cur[zc, yi + 1, here] + cur[zc, yi + 3, here])
                    + (cur[zc, yi + GAP, pl.ds(x0 - 1, chunk)] + cur[zc, yi + GAP, pl.ds(x0 + 1, chunk)])
                )
                far = (
                    (mids[zc - 2] + mids[zc + 2])
                    + (cur[zc, yi, here] + cur[zc, yi + 4, here])
                    + (cur[zc, yi + GAP, pl.ds(x0 - 2, chunk)] + cur[zc, yi + GAP, pl.ds(x0 + 2, chunk)])
                )
                r = coef[z, yi, pl.ds(x0 - PAD, chunk)] * v - K_NEAR * near + K_FAR * far
                if kind == "first":
                    r = 0.5 * r
                elif kind == "next":
                    r = r - out[zc, yi + GAP, here]
                else:
                    r = r * (1.0 / SCALE) + filter_center * v
                out[zc, yi + GAP, here] = r.astype(jnp.bfloat16).astype(jnp.float32)


def emit(buf, ref):
    @pl.loop(0, ref.shape[0])
    def _(z):
        cells = buf[z + 2, GAP : GAP + YB, PAD : PAD + NX].reshape(YB * NX, LANES)
        ref[z] = cells.T.astype(jnp.bfloat16)


def run_filter(orb_ref, rim_ref, pot_ref, f_ref, buf_a, buf_b, coef):
    planes = orb_ref.shape[0]
    count = orb_ref.shape[1]

    for k in range(4):
        z = k if k < 2 else planes + k
        rim = plane_in(rim_ref[k])
        buf_a[z, GAP : GAP + YB, PAD : PAD + NX] = rim
        buf_b[z, GAP : GAP + YB, PAD : PAD + NX] = rim

    @pl.loop(0, planes)
    def _(z):
        row = pot_ref[z].astype(jnp.float32)
        spread = jnp.broadcast_to((row - 1.75) * SCALE, (count, row.shape[-1]))
        coef[z] = plane_in(spread)
        buf_a[z + 2, GAP : GAP + YB, PAD : PAD + NX] = plane_in(orb_ref[z])
        fill_rims(buf_a, z + 2)

    def rims(buf):
        @pl.loop(0, planes)
        def _(z):
            fill_rims(buf, z + 2)

    cur, other = buf_a, buf_b
    apply_step(cur, other, coef, "first", planes)
    for _ in range(DEGREE - 1):
        cur, other = other, cur
        rims(cur)
        apply_step(cur, other, coef, "next", planes)
    cur, other = other, cur
    rims(cur)
    emit(cur, f_ref)
    return cur, other


def greet_all(barrier, bands, parts, band, part):
    total = bands * parts
    me = band * parts + part

    @pl.loop(1, total)
    def _(o):
        t = lax.rem(me + o, total)
        pl.semaphore_signal(
            barrier, inc=1, device_id=(t // parts, lax.rem(t, parts)), device_id_type=MESH
        )


def gram_kernel(
    bands, parts, total_cells,
    orb_ref, rim_ref, pot_ref, c_ref, p_ref,
    buf_a, buf_b, coef, f_ref, a_ref,
    all_f, own_a, blocks, landed,
    f_send, f_recv, a_send, a_recv, x_send, mate_send, local_sem, b_send, b_recv,
):
    band, part = lax.axis_index("band"), lax.axis_index("domain")
    lanes, cells = f_ref.shape[1:]
    groups = NY // YB
    count = lanes // groups
    rows = bands * count
    wide = rows // parts
    mate = part + 1 - 2 * lax.rem(part, 2)
    across = lax.rem(part + 2, parts)
    across_mate = lax.rem(mate + 2, parts)
    barrier = pltpu.get_barrier_semaphore()
    greet_all(barrier, bands, parts, band, part)
    cur, other = run_filter(orb_ref, rim_ref, pot_ref, f_ref, buf_a, buf_b, coef)
    pl.semaphore_wait(barrier, bands * parts - 1)

    core = lax.rem(part, 2)

    def turned(o, total):
        return o + core * (total - 2 * o)

    def band_copy(src, dst, send, recv, o, incoming, rows_at=slice(None)):
        o = turned(o, bands)
        peer = lax.rem(band + o, bands)
        source = lax.rem(band - o + bands, bands)
        slot = source if incoming else band
        return pltpu.make_async_remote_copy(
            src_ref=src.at[peer, rows_at], dst_ref=dst.at[slot, rows_at], send_sem=send.at[o],
            recv_sem=recv.at[slot], device_id=(peer, part), device_id_type=MESH,
        )

    def f_copy(o, incoming, rows_at=slice(None)):
        return band_copy(f_ref, all_f.at[part], f_send, f_recv.at[part], o, incoming, rows_at)

    def a_copy(o, incoming, rows_at=slice(None)):
        return band_copy(a_ref, own_a, a_send, a_recv, o, incoming, rows_at)

    def start_piece(copy, k):
        g, o = k // (bands - 1), 1 + lax.rem(k, bands - 1)
        copy(o, False, pl.ds(pl.multiple_of(g * count, count), count)).start()

    def from_band(o):
        return lax.rem(band - turned(o, bands) + bands, bands)

    def part_copy(owner, to, slot, send):
        return pltpu.make_async_remote_copy(
            src_ref=all_f.at[owner, slot], dst_ref=all_f.at[owner, slot], send_sem=send.at[slot],
            recv_sem=f_recv.at[owner, slot], device_id=(band, to), device_id_type=MESH,
        )

    keep_f = pltpu.make_async_copy(f_ref.at[band], all_f.at[part, band], local_sem.at[0])
    keep_f.start()

    @pl.loop(0, groups * (bands - 1))
    def _(k):
        start_piece(f_copy, k)

    keep_f.wait()
    part_copy(part, across, band, x_send).start()
    part_copy(part, mate, band, mate_send.at[0]).start()

    apply_step(cur, other, coef, "last", bands)
    emit(other, a_ref)
    keep_a = pltpu.make_async_copy(a_ref.at[band], own_a.at[band], local_sem.at[1])
    keep_a.start()

    @pl.loop(1, bands)
    def _(o):
        slot = from_band(o)
        f_copy(o, True).wait_recv()
        part_copy(part, across, slot, x_send).start()
        part_copy(part, mate, slot, mate_send.at[0]).start()
        for i in range(groups):
            start_piece(a_copy, (o - 1) * groups + i)

    @pl.loop(0, bands)
    def _(o):
        slot = lax.rem(from_band(o) + bands, bands)
        part_copy(across, mate, slot, mate_send.at[1]).wait_recv()
        part_copy(across, mate, slot, mate_send.at[1]).start()

    @pl.loop(0, bands)
    def _(slot):
        part_copy(mate, part, slot, mate_send.at[0]).wait_recv()
        part_copy(across_mate, part, slot, mate_send.at[1]).wait_recv()

    me = band * parts + part
    total_devices = bands * parts

    def block_copy(m, o, incoming, rows_at=slice(None)):
        o = turned(o, total_devices)
        t = lax.rem(me + o, total_devices)
        source = lax.rem(me - o + total_devices, total_devices)
        slot = source if incoming else me
        return pltpu.make_async_remote_copy(
            src_ref=blocks.at[m, t // parts, lax.rem(t, parts), rows_at],
            dst_ref=landed.at[m, slot, rows_at],
            send_sem=b_send.at[m, o], recv_sem=b_recv.at[m, slot],
            device_id=(t // parts, lax.rem(t, parts)), device_id_type=MESH,
        )

    def product(owner, columns):
        total = jnp.zeros((rows, rows), jnp.float32)
        for g in range(groups):
            at = slice(g * count, (g + 1) * count)
            total += lax.dot_general(
                all_f[owner, :, at].reshape(rows, cells),
                columns[:, at].reshape(rows, cells),
                (((1,), (1,)), ((), ())),
                preferred_element_type=jnp.float32,
            )
        return total

    def send_products(m, columns):
        @pl.loop(0, parts // 2)
        def _(p):
            pair = [product(2 * p + h, columns) for h in range(2)]
            at = pl.ds(pl.multiple_of(p * count, count), count)
            for k in range(parts):
                blocks[m, :, k, at] = jnp.concatenate(
                    [t[:, k * wide : (k + 1) * wide] for t in pair], axis=1
                ).reshape(bands, count, 2 * wide)

            @pl.loop(1, total_devices)
            def _(o):
                block_copy(m, o, False, at).start()

        keep = pltpu.make_async_copy(
            blocks.at[m, band, part], landed.at[m, me], local_sem.at[0]
        )
        keep.start()
        keep.wait()

    def finish(m, ref):
        @pl.loop(1, total_devices)
        def _(o):
            block_copy(m, o, True).wait_recv()

        sums = []
        for d in range(parts):
            total = landed[m, d]
            for b in range(1, bands):
                total = total + landed[m, b * parts + d]
            sums.append(total * (1.0 / total_cells))
        for k in range(parts):
            p, h = k // 2, k % 2
            ref[k * count : (k + 1) * count] = jnp.concatenate(
                [
                    sums[d][p * count : (p + 1) * count, h * wide + j * count : h * wide + (j + 1) * count]
                    for j in range(bands // parts)
                    for d in range(parts)
                ],
                axis=1,
            )

    send_products(0, all_f.at[part])
    keep_a.wait()

    @pl.loop(1, bands)
    def _(o):
        a_copy(o, True).wait_recv()

    send_products(1, own_a)
    finish(0, c_ref)
    finish(1, p_ref)

    @pl.loop(1, bands)
    def _(o):
        f_copy(o, False).wait_send()
        a_copy(o, False).wait_send()

    @pl.loop(0, bands)
    def _(slot):
        part_copy(part, across, slot, x_send).wait_send()
        part_copy(part, mate, slot, mate_send.at[0]).wait_send()
        part_copy(across, mate, slot, mate_send.at[1]).wait_send()

    @pl.loop(1, total_devices)
    def _(o):
        block_copy(0, o, False).wait_send()
        block_copy(1, o, False).wait_send()


def run_all(orb, rim, pot, bands, parts, total_cells):
    planes, count = orb.shape[:2]
    whole = pl.BlockSpec(memory_space=pltpu.VMEM)
    dma = pltpu.SemaphoreType.DMA
    lanes, cells = LANES, YB * NX
    orb_count = count * parts
    block = (orb_count // 2, 2 * bands * count // parts)
    field = pltpu.VMEM((planes + 4, YB + 2 * GAP, NX + 2 * PAD, LANES), jnp.float32)
    pieces = pltpu.VMEM((planes, lanes, cells), jnp.bfloat16)
    out = jax.ShapeDtypeStruct((orb_count, bands * orb_count // parts), jnp.float32)
    dma = pltpu.SemaphoreType.DMA
    return pl.pallas_call(
        functools.partial(gram_kernel, bands, parts, total_cells),
        out_shape=(out, out),
        in_specs=[whole] * 3,
        out_specs=(whole, whole),
        scratch_shapes=[
            field, field, pltpu.VMEM((planes, YB, NX, LANES), jnp.float32), pieces, pieces,
            pltpu.VMEM((parts, bands, lanes, cells), jnp.bfloat16),
            pltpu.VMEM((bands, lanes, cells), jnp.bfloat16),
            pltpu.VMEM((2, bands, parts, *block), jnp.float32),
            pltpu.VMEM((2, bands * parts, *block), jnp.float32),
            dma((bands,)), dma((parts, bands)), dma((bands,)), dma((bands,)),
            dma((bands,)), dma((2, bands)), dma((2,)),
            dma((2, bands * parts)), dma((2, bands * parts)),
        ],
        compiler_params=pltpu.CompilerParams(
            collective_id=0, has_side_effects=True, vmem_limit_bytes=60 * 1024 * 1024
        ),
        name="filter_and_gram",
    )(orb, rim, pot[:, None])


def whole_orbitals(orbitals, boundary, potential):
    orb_count, planes_here, plane = orbitals.shape
    parts = lax.axis_size("domain")
    bands = lax.axis_size("band")
    part = lax.axis_index("domain")
    count = orb_count // parts

    split = orbitals.reshape(parts, count, planes_here, plane).transpose(0, 2, 1, 3)
    mine = lax.all_to_all(split, "domain", split_axis=0, concat_axis=0, tiled=True)
    mine = mine.reshape(parts * planes_here, count, plane)
    rim = lax.dynamic_slice_in_dim(boundary, part * count, count, 0).transpose(1, 0, 2)
    rim, potential = lax.optimization_barrier((rim, potential))
    pot = lax.all_gather(potential, "domain", axis=0, tiled=True)
    return run_all(mine, rim, pot, bands, parts, parts * planes_here * plane)


def solution(mesh):
    parts, bands = mesh.shape["domain"], mesh.shape["band"]

    def body(orbitals, boundary, potential):
        fits = (
            orbitals.shape[0] * (NY // YB) == LANES * parts
            and orbitals.shape[1] * parts == bands
            and bands % parts == 0
            and parts == 4
        )
        return (whole_orbitals if fits else per_device)(orbitals, boundary, potential)

    return jax.shard_map(
        body,
        mesh=mesh,
        in_specs=(P("band", "domain", None), P("band", None, None), P("domain", None)),
        out_specs=(P("band", "domain"), P("band", "domain")),
        check_vma=False,
    )
```

```python
import functools

import jax
import jax.numpy as jnp
from jax import lax
from jax.experimental import pallas as pl
from jax.experimental.pallas import tpu as pltpu
from jax.sharding import PartitionSpec as P

NX = 160
NY = 32
NZ_DEV = 2
DEGREE = 4
LANES = 128
PAD = 8
YB = 8
GAP = 2
MESH = pl.DeviceIdType.MESH


filter_center = 5.5
filter_radius = 4.5


def padded_2(cells, sides, width):
    for axis, dim in sides:
        count = lax.axis_size(axis)
        ends = count - 1
        head = lax.slice_in_dim(cells, 0, width, axis=dim)
        tail = lax.slice_in_dim(cells, cells.shape[dim] - width, cells.shape[dim], axis=dim)
        cells = jnp.concatenate(
            [
                lax.ppermute(tail, axis, [(i, (i + 1) % count) for i in range(ends)]),
                cells,
                lax.ppermute(head, axis, [((i + 1) % count, i) for i in range(ends)]),
            ],
            axis=dim,
        )
    return cells


def second_diff(values, axis_pos):
    near = jnp.roll(values, 1, axis_pos) + jnp.roll(values, -1, axis_pos)
    far = jnp.roll(values, 2, axis_pos) + jnp.roll(values, -2, axis_pos)
    return (16.0 * near - far - 30.0 * values) / 12.0


def plane_part(values):
    shaped = values.reshape(values.shape[:-1] + (NY, NX))
    total = second_diff(shaped, -1) + second_diff(shaped, -2)
    return total.reshape(values.shape)


def hamiltonian(padded, potential):
    middle = padded[:, 2:-2]
    z_part = (
        16.0 * (padded[:, 1:-3] + padded[:, 3:-1])
        - (padded[:, :-4] + padded[:, 4:])
        - 30.0 * middle
    ) / 12.0
    laplace = z_part + plane_part(middle)
    return -0.5 * laplace + potential.astype(jnp.float32) * middle


def chebyshev(apply_ham, orb_block):
    earlier = orb_block
    current = (
        (apply_ham(orb_block) - filter_center * orb_block.astype(jnp.float32)) / filter_radius
    ).astype(jnp.bfloat16)
    for degree_step in range(DEGREE - 1):
        following = (
            2.0 * (apply_ham(current) - filter_center * current.astype(jnp.float32)) / filter_radius
        )
        following = (following - earlier.astype(jnp.float32)).astype(jnp.bfloat16)
        earlier, current = (current, following)
    return (current, apply_ham(current).astype(jnp.bfloat16))


def per_device(orbitals, boundary, potential):
    orb_count = orbitals.shape[0]
    domain_pos = lax.axis_index("domain")
    domain_count = lax.axis_size("domain")
    last_pos = domain_count - 1

    def apply_ham(values):
        padded = padded_2(values, (("domain", 1),), 2)
        lower_rim = jnp.where(domain_pos == 0, boundary[:, 0:2], padded[:, 0:2])
        upper_rim = jnp.where(domain_pos == last_pos, boundary[:, 2:4], padded[:, -2:])
        padded = jnp.concatenate([lower_rim, padded[:, 2:-2], upper_rim], axis=1).astype(
            jnp.float32
        )
        return hamiltonian(padded, potential)

    filtered, applied = chebyshev(apply_ham, orbitals)
    filtered = filtered.reshape(orb_count, -1)
    applied = applied.reshape(orb_count, -1)
    cell_y, cell_h = (
        lax.all_to_all(filtered, "band", split_axis=1, concat_axis=0, tiled=True),
        lax.all_to_all(applied, "band", split_axis=1, concat_axis=0, tiled=True),
    )
    cell_y, cell_h = (
        lax.all_gather(cell_y, "domain", axis=1, tiled=True),
        lax.all_gather(cell_h, "domain", axis=1, tiled=True),
    )
    column_count = cell_y.shape[0] // domain_count
    column_y = lax.dynamic_slice_in_dim(cell_y, domain_pos * column_count, column_count, 0)
    column_h = lax.dynamic_slice_in_dim(cell_h, domain_pos * column_count, column_count, 0)
    contract_dims = (((1,), (1,)), ((), ()))
    with_y = lax.dot_general(cell_y, column_y, contract_dims, preferred_element_type=jnp.float32)
    with_h = lax.dot_general(cell_y, column_h, contract_dims, preferred_element_type=jnp.float32)
    summed = lax.psum_scatter(
        jnp.concatenate([with_y, with_h], axis=1), "band", scatter_dimension=0, tiled=True
    )
    total_cells = NZ_DEV * NY * NX * domain_count
    correlation = summed[:, :column_count] / total_cells
    projected = summed[:, column_count:] / total_cells
    return (correlation, projected)


SCALE = 2.0 / filter_radius
K_NEAR = SCALE * 16.0 / 24.0
K_FAR = SCALE / 24.0


def plane_in(src):
    group = YB * NX
    rows = jnp.concatenate(
        [src[:, g * group : (g + 1) * group].astype(jnp.float32) for g in range(NY // YB)], axis=0
    )
    return rows.T.reshape(YB, NX, LANES)


def fill_rims(buf, z):
    for yi in range(YB):
        buf[z, yi + GAP, PAD - 2 : PAD] = buf[z, yi + GAP, PAD + NX - 2 : PAD + NX]
        buf[z, yi + GAP, PAD + NX : PAD + NX + 2] = buf[z, yi + GAP, PAD : PAD + 2]
    turn = LANES // (NY // YB)
    for k in range(GAP):
        low = buf[z, YB + k, PAD : PAD + NX]
        buf[z, k, PAD : PAD + NX] = pltpu.roll(low, turn, 1)
        high = buf[z, GAP + k, PAD : PAD + NX]
        buf[z, GAP + YB + k, PAD : PAD + NX] = pltpu.roll(high, LANES - turn, 1)


def apply_step(cur, out, coef, kind, planes):
    chunk = 16

    @pl.loop(0, YB)
    def _(yi):
        for x0 in range(PAD, PAD + NX, chunk):
            here = pl.ds(x0, chunk)
            mids = [cur[z, yi + GAP, here] for z in range(planes + 4)]
            for z in range(planes):
                zc = z + 2
                v = mids[zc]
                near = (
                    (mids[zc - 1] + mids[zc + 1])
                    + (cur[zc, yi + 1, here] + cur[zc, yi + 3, here])
                    + (cur[zc, yi + GAP, pl.ds(x0 - 1, chunk)] + cur[zc, yi + GAP, pl.ds(x0 + 1, chunk)])
                )
                far = (
                    (mids[zc - 2] + mids[zc + 2])
                    + (cur[zc, yi, here] + cur[zc, yi + 4, here])
                    + (cur[zc, yi + GAP, pl.ds(x0 - 2, chunk)] + cur[zc, yi + GAP, pl.ds(x0 + 2, chunk)])
                )
                r = coef[z, yi, pl.ds(x0 - PAD, chunk)] * v - K_NEAR * near + K_FAR * far
                if kind == "first":
                    r = 0.5 * r
                elif kind == "next":
                    r = r - out[zc, yi + GAP, here]
                else:
                    r = r * (1.0 / SCALE) + filter_center * v
                out[zc, yi + GAP, here] = r.astype(jnp.bfloat16).astype(jnp.float32)


def emit(buf, ref):
    @pl.loop(0, ref.shape[0])
    def _(z):
        cells = buf[z + 2, GAP : GAP + YB, PAD : PAD + NX].reshape(YB * NX, LANES)
        ref[z] = cells.T.astype(jnp.bfloat16)


def run_filter(orb_ref, rim_ref, pot_ref, f_ref, buf_a, buf_b, coef):
    planes = orb_ref.shape[0]
    count = orb_ref.shape[1]

    for k in range(4):
        z = k if k < 2 else planes + k
        rim = plane_in(rim_ref[k])
        buf_a[z, GAP : GAP + YB, PAD : PAD + NX] = rim
        buf_b[z, GAP : GAP + YB, PAD : PAD + NX] = rim

    @pl.loop(0, planes)
    def _(z):
        row = pot_ref[z].astype(jnp.float32)
        spread = jnp.broadcast_to((row - 1.75) * SCALE, (count, row.shape[-1]))
        coef[z] = plane_in(spread)
        buf_a[z + 2, GAP : GAP + YB, PAD : PAD + NX] = plane_in(orb_ref[z])
        fill_rims(buf_a, z + 2)

    def rims(buf):
        @pl.loop(0, planes)
        def _(z):
            fill_rims(buf, z + 2)

    cur, other = buf_a, buf_b
    apply_step(cur, other, coef, "first", planes)
    for _ in range(DEGREE - 1):
        cur, other = other, cur
        rims(cur)
        apply_step(cur, other, coef, "next", planes)
    cur, other = other, cur
    rims(cur)
    emit(cur, f_ref)
    return cur, other


def greet_all(barrier, bands, parts, band, part):
    total = bands * parts
    me = band * parts + part

    @pl.loop(1, total)
    def _(o):
        t = lax.rem(me + o, total)
        pl.semaphore_signal(
            barrier, inc=1, device_id=(t // parts, lax.rem(t, parts)), device_id_type=MESH
        )


def gram_kernel(
    bands, parts, total_cells,
    orb_ref, rim_ref, pot_ref, c_ref, p_ref,
    buf_a, buf_b, coef, f_ref, a_ref,
    all_f, own_a, blocks, landed,
    f_send, f_recv, a_send, a_recv, x_send, mate_send, local_sem, b_send, b_recv,
):
    band, part = lax.axis_index("band"), lax.axis_index("domain")
    lanes, cells = f_ref.shape[1:]
    groups = NY // YB
    count = lanes // groups
    rows = bands * count
    wide = rows // parts
    mate = part + 1 - 2 * lax.rem(part, 2)
    across = lax.rem(part + 2, parts)
    across_mate = lax.rem(mate + 2, parts)
    barrier = pltpu.get_barrier_semaphore()
    greet_all(barrier, bands, parts, band, part)
    cur, other = run_filter(orb_ref, rim_ref, pot_ref, f_ref, buf_a, buf_b, coef)
    pl.semaphore_wait(barrier, bands * parts - 1)

    core = lax.rem(part, 2)

    def turned(o, total):
        return o + core * (total - 2 * o)

    def band_copy(src, dst, send, recv, o, incoming, rows_at=slice(None)):
        o = turned(o, bands)
        peer = lax.rem(band + o, bands)
        source = lax.rem(band - o + bands, bands)
        slot = source if incoming else band
        return pltpu.make_async_remote_copy(
            src_ref=src.at[peer, rows_at], dst_ref=dst.at[slot, rows_at], send_sem=send.at[o],
            recv_sem=recv.at[slot], device_id=(peer, part), device_id_type=MESH,
        )

    def f_copy(o, incoming, rows_at=slice(None)):
        return band_copy(f_ref, all_f.at[part], f_send, f_recv.at[part], o, incoming, rows_at)

    def a_copy(o, incoming, rows_at=slice(None)):
        return band_copy(a_ref, own_a, a_send, a_recv, o, incoming, rows_at)

    def start_piece(copy, k):
        g, o = k // (bands - 1), 1 + lax.rem(k, bands - 1)
        copy(o, False, pl.ds(pl.multiple_of(g * count, count), count)).start()

    def from_band(o):
        return lax.rem(band - turned(o, bands) + bands, bands)

    def part_copy(owner, to, slot, send):
        return pltpu.make_async_remote_copy(
            src_ref=all_f.at[owner, slot], dst_ref=all_f.at[owner, slot], send_sem=send.at[slot],
            recv_sem=f_recv.at[owner, slot], device_id=(band, to), device_id_type=MESH,
        )

    keep_f = pltpu.make_async_copy(f_ref.at[band], all_f.at[part, band], local_sem.at[0])
    keep_f.start()

    @pl.loop(0, groups * (bands - 1))
    def _(k):
        start_piece(f_copy, k)

    keep_f.wait()
    part_copy(part, across, band, x_send).start()
    part_copy(part, mate, band, mate_send.at[0]).start()

    apply_step(cur, other, coef, "last", bands)
    emit(other, a_ref)
    keep_a = pltpu.make_async_copy(a_ref.at[band], own_a.at[band], local_sem.at[1])
    keep_a.start()

    @pl.loop(1, bands)
    def _(o):
        slot = from_band(o)
        f_copy(o, True).wait_recv()
        part_copy(part, across, slot, x_send).start()
        part_copy(part, mate, slot, mate_send.at[0]).start()
        for i in range(groups):
            start_piece(a_copy, (o - 1) * groups + i)

    @pl.loop(0, bands)
    def _(o):
        slot = lax.rem(from_band(o) + bands, bands)
        part_copy(across, mate, slot, mate_send.at[1]).wait_recv()
        part_copy(across, mate, slot, mate_send.at[1]).start()

    @pl.loop(0, bands)
    def _(slot):
        part_copy(mate, part, slot, mate_send.at[0]).wait_recv()
        part_copy(across_mate, part, slot, mate_send.at[1]).wait_recv()

    me = band * parts + part
    total_devices = bands * parts

    def block_copy(m, o, incoming, rows_at=slice(None)):
        o = turned(o, total_devices)
        t = lax.rem(me + o, total_devices)
        source = lax.rem(me - o + total_devices, total_devices)
        slot = source if incoming else me
        return pltpu.make_async_remote_copy(
            src_ref=blocks.at[m, t // parts, lax.rem(t, parts), rows_at],
            dst_ref=landed.at[m, slot, rows_at],
            send_sem=b_send.at[m, o], recv_sem=b_recv.at[m, slot],
            device_id=(t // parts, lax.rem(t, parts)), device_id_type=MESH,
        )

    def product(owner, columns):
        total = jnp.zeros((rows, rows), jnp.float32)
        for g in range(groups):
            at = slice(g * count, (g + 1) * count)
            total += lax.dot_general(
                all_f[owner, :, at].reshape(rows, cells),
                columns[:, at].reshape(rows, cells),
                (((1,), (1,)), ((), ())),
                preferred_element_type=jnp.float32,
            )
        return total

    def send_products(m, columns):
        @pl.loop(0, parts // 2)
        def _(p):
            pair = [product(2 * p + h, columns) for h in range(2)]
            at = pl.ds(pl.multiple_of(p * count, count), count)
            for k in range(parts):
                blocks[m, :, k, at] = jnp.concatenate(
                    [t[:, k * wide : (k + 1) * wide] for t in pair], axis=1
                ).reshape(bands, count, 2 * wide)

            @pl.loop(1, total_devices)
            def _(o):
                block_copy(m, o, False, at).start()

        keep = pltpu.make_async_copy(
            blocks.at[m, band, part], landed.at[m, me], local_sem.at[0]
        )
        keep.start()
        keep.wait()

    def finish(m, ref):
        @pl.loop(1, total_devices)
        def _(o):
            block_copy(m, o, True).wait_recv()

        sums = []
        for d in range(parts):
            total = landed[m, d]
            for b in range(1, bands):
                total = total + landed[m, b * parts + d]
            sums.append(total * (1.0 / total_cells))
        for k in range(parts):
            p, h = k // 2, k % 2
            ref[k * count : (k + 1) * count] = jnp.concatenate(
                [
                    sums[d][p * count : (p + 1) * count, h * wide + j * count : h * wide + (j + 1) * count]
                    for j in range(bands // parts)
                    for d in range(parts)
                ],
                axis=1,
            )

    send_products(0, all_f.at[part])
    keep_a.wait()

    @pl.loop(1, bands)
    def _(o):
        a_copy(o, True).wait_recv()

    send_products(1, own_a)
    finish(0, c_ref)
    finish(1, p_ref)

    @pl.loop(1, bands)
    def _(o):
        f_copy(o, False).wait_send()
        a_copy(o, False).wait_send()

    @pl.loop(0, bands)
    def _(slot):
        part_copy(part, across, slot, x_send).wait_send()
        part_copy(part, mate, slot, mate_send.at[0]).wait_send()
        part_copy(across, mate, slot, mate_send.at[1]).wait_send()

    @pl.loop(1, total_devices)
    def _(o):
        block_copy(0, o, False).wait_send()
        block_copy(1, o, False).wait_send()


def run_all(orb, rim, pot, bands, parts, total_cells):
    planes, count = orb.shape[:2]
    whole = pl.BlockSpec(memory_space=pltpu.VMEM)
    dma = pltpu.SemaphoreType.DMA
    lanes, cells = LANES, YB * NX
    orb_count = count * parts
    block = (orb_count // 2, 2 * bands * count // parts)
    field = pltpu.VMEM((planes + 4, YB + 2 * GAP, NX + 2 * PAD, LANES), jnp.float32)
    pieces = pltpu.VMEM((planes, lanes, cells), jnp.bfloat16)
    out = jax.ShapeDtypeStruct((orb_count, bands * orb_count // parts), jnp.float32)
    dma = pltpu.SemaphoreType.DMA
    return pl.pallas_call(
        functools.partial(gram_kernel, bands, parts, total_cells),
        out_shape=(out, out),
        in_specs=[whole] * 3,
        out_specs=(whole, whole),
        scratch_shapes=[
            field, field, pltpu.VMEM((planes, YB, NX, LANES), jnp.float32), pieces, pieces,
            pltpu.VMEM((parts, bands, lanes, cells), jnp.bfloat16),
            pltpu.VMEM((bands, lanes, cells), jnp.bfloat16),
            pltpu.VMEM((2, bands, parts, *block), jnp.float32),
            pltpu.VMEM((2, bands * parts, *block), jnp.float32),
            dma((bands,)), dma((parts, bands)), dma((bands,)), dma((bands,)),
            dma((bands,)), dma((2, bands)), dma((2,)),
            dma((2, bands * parts)), dma((2, bands * parts)),
        ],
        compiler_params=pltpu.CompilerParams(
            collective_id=0, has_side_effects=True, vmem_limit_bytes=60 * 1024 * 1024
        ),
        name="filter_and_gram",
    )(orb, rim, pot[:, None])


def whole_orbitals(orbitals, boundary, potential):
    orb_count, planes_here, plane = orbitals.shape
    parts = lax.axis_size("domain")
    bands = lax.axis_size("band")
    part = lax.axis_index("domain")
    count = orb_count // parts

    split = orbitals.reshape(parts, count, planes_here, plane).transpose(0, 2, 1, 3)
    mine = lax.all_to_all(split, "domain", split_axis=0, concat_axis=0, tiled=True)
    mine = mine.reshape(parts * planes_here, count, plane)
    rim = lax.dynamic_slice_in_dim(boundary, part * count, count, 0).transpose(1, 0, 2)
    rim, potential = lax.optimization_barrier((rim, potential))
    pot = lax.all_gather(potential, "domain", axis=0, tiled=True)
    return run_all(mine, rim, pot, bands, parts, parts * planes_here * plane)


def solution(mesh):
    parts, bands = mesh.shape["domain"], mesh.shape["band"]

    def body(orbitals, boundary, potential):
        fits = (
            orbitals.shape[0] * (NY // YB) == LANES * parts
            and orbitals.shape[1] * parts == bands
            and bands % parts == 0
            and parts == 4
        )
        return (whole_orbitals if fits else per_device)(orbitals, boundary, potential)

    return jax.shard_map(
        body,
        mesh=mesh,
        in_specs=(P("band", "domain", None), P("band", None, None), P("domain", None)),
        out_specs=(P("band", "domain"), P("band", "domain")),
        check_vma=False,
    )
```
